512 devices in a mesh: lon: 64 (over y, z_hi, core), lat: 8 (over x, z_lo).
Axes of the slice: x: 4, y: 8, z: 8 (z_hi: 4, z_lo: 2; z = z_hi * 2 + z_lo), core: 2. Of those that a mesh axis runs over, the one named last changes fastest.
Arguments:
- state_field: float32 [48, 2048, 1024], P(None, 'lon', 'lat'), may hold values from -6 to 6
- weight_bank: float32 [9, 48, 48], replicated, may hold values from -0.3125 to 0.3125
- cotangent: float32 [48, 2048, 1024], P(None, 'lon', 'lat'), may hold values from -6 to 6
Outputs:
- response: float32 [48, 2048, 1024], P(None, 'lon', 'lat')
- grad_field: float32 [48, 2048, 1024], P(None, 'lon', 'lat')
- grad_weight: float32 [9, 48, 48], replicated
The draws below stay inside these ranges and needn't reach their ends.
All inputs are finite; a program needn't handle non-finite values.
Results may differ from the reference program's by a relative error of at most 0.0003.
Values sent between devices are 32-bit elements; how exact they have to be, the bound alone decides.
A program may use at most 64 MiB of HBM per device.

```python
import math
import jax
import jax.numpy as jnp
from jax import lax

CHANNELS = 48
NLAT = 1024
NLON = 2048


def level_of(key, extent, pieces, low, largest):
    factor_of = 1.0
    for position, blocks in pieces:
        steps = jax.random.uniform(jax.random.fold_in(jax.random.fold_in(key, 6), position), (blocks,), jnp.float32, low / len(pieces), largest / len(pieces))
        factor_of = factor_of * jnp.repeat(jnp.exp(steps), extent[position] // blocks).reshape((-1,) + (1,) * (len(extent) - 1 - position))
    return factor_of


def gaussian(rng, dims, deviation, reach, shards=(), kind=jnp.bfloat16):
    drawn = deviation * jax.random.normal(rng, dims, jnp.float32)
    if shards:
        drawn = drawn * level_of(rng, dims, shards, -0.22, 0.18)
    return jnp.clip(drawn, -reach, reach).astype(kind)


def setup_inputs(seed: int = 0) -> dict:
    arg_keys = jax.random.split(jax.random.key(seed), 4)
    state_field = gaussian(arg_keys[0], (CHANNELS, NLON, NLAT), 1.0, 6.0, ((1, 64), (2, 8)), jnp.float32)
    weight_bank = gaussian(arg_keys[1], (9, CHANNELS, CHANNELS), (9 * CHANNELS) ** -0.5, 0.3125, (), jnp.float32)
    cotangent = gaussian(arg_keys[2], (CHANNELS, NLON, NLAT), 1.0, 6.0, ((1, 64), (2, 8)), jnp.float32)
    return {"state_field": state_field, "weight_bank": weight_bank, "cotangent": cotangent}


def extend_grid(values):
    half_turn = NLON // 2
    north_row = jnp.roll(values[:, :, :1], -half_turn, axis=1)
    south_row = jnp.roll(values[:, :, -1:], -half_turn, axis=1)
    banded = jnp.concatenate([north_row, values, south_row], axis=2)
    return jnp.concatenate([banded[:, -1:, :], banded, banded[:, :1, :]], axis=1)

def apply_layer(state_field, weight_bank):
    kernel = weight_bank.reshape(3, 3, CHANNELS, CHANNELS).transpose(2, 3, 1, 0)
    padded = extend_grid(state_field)
    return lax.conv_general_dilated(padded[None], kernel, (1, 1), 'VALID', precision=lax.Precision.HIGHEST)[0]

def reference(state_field, weight_bank, cotangent):
    response, pullback = jax.vjp(apply_layer, state_field, weight_bank)
    grad_field, grad_weight = pullback(cotangent)
    factor = 1.0 / math.sqrt(NLAT * NLON)
    return (response, grad_field, grad_weight * factor)
```

```python
import functools
import math

import jax
import jax.numpy as jnp
from jax import lax
from jax.experimental import pallas as pl
from jax.experimental.pallas import tpu as pltpu
from jax.sharding import PartitionSpec as P

CH = 48
COLS = 32
ROWS = 128
PART = 24
MESH = pl.DeviceIdType.MESH
F32 = jnp.float32
BF16 = jnp.bfloat16


def split(x):
    hi = x.astype(BF16)
    return hi, (x - hi.astype(F32)).astype(BF16)


def column(ref, j):
    return ref[pl.ds(j, CH, stride=COLS), :]


def dot_nn(a, b):
    return lax.dot_general(a, b, (((1,), (0,)), ((), ())), preferred_element_type=F32)


def dot_nt(a, b):
    return lax.dot_general(a, b, (((1,), (1,)), ((), ())), preferred_element_type=F32)


def remote(src, dst, send, recv, to):
    return pltpu.make_async_remote_copy(
        src_ref=src, dst_ref=dst, send_sem=send, recv_sem=recv,
        device_id=to, device_id_type=MESH,
    )


def kernel(scale, f_hbm, g_hbm, w_ref, resp_ref, gfield_ref, gw_ref,
           fv, gv, z, v, p, edge, halo, colout, colin, corner, cornerin,
           part, got, total, whole, in_sem, hs_sem, hr_sem, as_sem, ar_sem):
    lon = lax.axis_index("lon")
    lat = lax.axis_index("lat")
    n_lon = lax.axis_size("lon")
    n_lat = lax.axis_size("lat")
    y, zh, core = lon // 8, (lon // 2) % 4, lon % 2
    x, zl = lat // 2, lat % 2
    depth = zh * 2 + zl
    is_north = jnp.where(lat == 0, 1, 0)
    is_south = jnp.where(lat == n_lat - 1, 1, 0)
    opposite = (lon + n_lon // 2) % n_lon

    def place(x, y, depth, core):
        return (y * 8 + (depth // 2) * 2 + core, x * 2 + depth % 2)

    west = ((lon + n_lon - 1) % n_lon, lat)
    east = ((lon + 1) % n_lon, lat)
    north = (jnp.where(lat == 0, opposite, lon), jnp.where(lat == 0, 0, lat - 1))
    south = (jnp.where(lat == n_lat - 1, opposite, lon),
             jnp.where(lat == n_lat - 1, n_lat - 1, lat + 1))
    near = [(dx, dc) for dx in range(4) for dc in range(2) if (dx, dc) != (0, 0)]
    pool = [place((x + dx) % 4, y, depth, (core + dc) % 2) for dx, dc in near]
    pool_rank = [((x + dx) % 4) * 2 + (core + dc) % 2 for dx, dc in near]
    along_y = [place(x, (y + k) % 8, depth, core) for k in range(1, 8)]
    along_z = [place(x, y, (depth + k) % 8, core) for k in range(1, 8)]
    rank = x * 2 + core

    barrier = pltpu.get_barrier_semaphore()
    partners = [west, east, north, south] + pool + along_y + along_z
    for to in partners:
        pl.semaphore_signal(barrier, inc=1, device_id=to, device_id_type=MESH)
    load_f = pltpu.make_async_copy(f_hbm, fv, in_sem.at[0])
    load_g = pltpu.make_async_copy(g_hbm, gv, in_sem.at[1])
    load_f.start()
    load_g.start()
    v[0] = jnp.zeros((6 * CH, ROWS), BF16)
    v[COLS + 1] = jnp.zeros((6 * CH, ROWS), BF16)
    load_f.wait()
    load_g.wait()

    lane = lax.broadcasted_iota(jnp.int32, (CH, ROWS), 1)

    def pack(j, acc):
        acc = jnp.where(lane // 2 == j, pltpu.roll(column(fv, j), 2 * j + 1, 1), acc)
        return jnp.where(lane // 2 == j + 32, pltpu.roll(column(gv, j), (2 * j + 65) % 128, 1), acc)

    edge[...] = lax.fori_loop(0, COLS, pack, jnp.zeros((CH, ROWS), F32))
    for side, j in enumerate((0, COLS - 1)):
        colout[side, :CH] = column(fv, j)
        colout[side, CH:] = column(gv, j)

    pl.semaphore_wait(barrier, len(partners))

    from_north = jnp.where(lat == 0, 0, 1)
    from_south = jnp.where(lat == n_lat - 1, 1, 0)
    halo_out = [
        remote(edge, halo.at[from_north], hs_sem.at[0], hr_sem.at[from_north], north),
        remote(edge, halo.at[from_south], hs_sem.at[1], hr_sem.at[from_south], south),
        remote(colout.at[0], colin.at[1], hs_sem.at[2], hr_sem.at[3], west),
        remote(colout.at[1], colin.at[0], hs_sem.at[3], hr_sem.at[2], east),
    ]
    for copy in halo_out:
        copy.start()

    def put(ref, at, a, value):
        hi, lo = split(value)
        ref[at, a * CH:(a + 1) * CH] = hi
        ref[at, (3 + a) * CH:(4 + a) * CH] = lo

    def shifted_down(value):
        return jnp.where(lane == 0, 0.0, pltpu.roll(value, 1, 1))

    def shifted_up(value):
        return jnp.where(lane == ROWS - 1, 0.0, pltpu.roll(value, ROWS - 1, 1))

    def build_plain(value, at):
        put(z, at, 0, shifted_down(value))
        put(z, at, 1, value)
        put(z, at, 2, shifted_up(value))

    def first_build(j, carry):
        build_plain(column(fv, j), j + 1)
        put(v, j + 1, 1, column(gv, j))
        return carry

    lax.fori_loop(0, COLS, first_build, 0)

    def weight_step(lhs_hi, lhs_lo, rhs_hi, rhs_lo):
        return dot_nt(lhs_hi, rhs_hi) + dot_nt(lhs_lo, rhs_hi) + dot_nt(lhs_hi, rhs_lo)

    def local_weight(s, acc):
        sides = [[], [], [], []]
        for k in range(4):
            at = s * 4 + k + 1
            for low in range(2):
                r = (1 + 3 * low) * CH
                sides[low].append(jnp.concatenate(
                    [v[at + 1, r:r + CH], v[at, r:r + CH], v[at - 1, r:r + CH]], axis=0))
                sides[2 + low].append(z[at, 3 * CH * low:3 * CH * (low + 1)])
        return acc + weight_step(*[jnp.concatenate(s, axis=1) for s in sides])

    acc = lax.fori_loop(0, COLS // 4, local_weight, jnp.zeros((3 * CH, 3 * CH), F32))

    forward = jnp.concatenate(
        [jnp.concatenate([w_ref[3 * a + b] for a in range(3)], axis=1) for b in range(3)], axis=0)
    turned = jnp.concatenate(
        [jnp.concatenate([w_ref[3 * (2 - a) + 2 - b] for b in range(3)], axis=1) for a in range(3)], axis=0)
    turned = jnp.concatenate([turned, jnp.zeros((3 * CH, 256 - 3 * CH), F32)], axis=1)
    turned = jnp.concatenate([turned, jnp.zeros((256 - 3 * CH, 256), F32)], axis=0)
    adjoint = turned.T[:3 * CH, :3 * CH]
    fwd_hi, fwd_lo = split(forward)
    adj_hi, adj_lo = split(adjoint)

    remote(edge, halo.at[0], hs_sem.at[0], hr_sem.at[0], north).wait_recv()
    remote(edge, halo.at[1], hs_sem.at[1], hr_sem.at[1], south).wait_recv()
    beyond = jnp.where(
        lane % 2 == 0,
        pltpu.roll(halo[1], 1 + is_south, 1),
        pltpu.roll(halo[0], 3 - is_north, 1),
    )
    corner[...] = beyond
    remote(colout.at[0], colin.at[1], hs_sem.at[2], hr_sem.at[3], west).wait_recv()
    remote(colout.at[1], colin.at[0], hs_sem.at[3], hr_sem.at[2], east).wait_recv()

    build_plain(colin[0, :CH], 0)
    build_plain(colin[1, :CH], COLS + 1)
    blank = jnp.zeros((CH, ROWS), BF16)
    outer = []
    for low in range(2):
        r = (1 + 3 * low) * CH
        outer.append(jnp.concatenate([
            jnp.concatenate([v[1, r:r + CH], blank], axis=1),
            jnp.concatenate([blank, blank], axis=1),
            jnp.concatenate([blank, v[COLS, r:r + CH]], axis=1)], axis=0))
    for low in range(2):
        r = 3 * CH * low
        outer.append(jnp.concatenate([z[0, r:r + 3 * CH], z[COLS + 1, r:r + 3 * CH]], axis=1))
    acc = acc + weight_step(*outer)

    def packed(value, left):
        hi = value.astype(BF16).astype(F32)
        lo = (value - hi).astype(BF16).astype(F32)
        first, second = (lo, hi) if left else (hi, lo)
        return jnp.concatenate([hi + pltpu.roll(first, 64, 1), second], axis=1).astype(BF16)

    own = edge[...]
    inside = lane < 64
    left_rows = []
    for b in (-1, 0, 1):
        value = pltpu.roll(own, (64 + 2 * b) % 128, 1)
        if b == 1:
            value = jnp.where(lane < 2, pltpu.roll(colin[0, CH:], 1, 1), value)
        if b == -1:
            value = jnp.where(lane >= 62, pltpu.roll(colin[1, CH:], 63, 1), value)
        left_rows.append(packed(jnp.where(inside, value, 0.0), True))
    across = pltpu.roll(beyond, 126, 1)
    right_rows = [
        packed(jnp.where(inside & (lane % 2 == 1), across, 0.0), False),
        jnp.zeros((CH, 256), BF16),
        packed(jnp.where(inside & (lane % 2 == 0), across, 0.0), False),
    ]
    acc = acc + dot_nt(jnp.concatenate(left_rows, axis=0), jnp.concatenate(right_rows, axis=0))

    part[:3 * CH] = acc[:, :128]
    tail = jnp.concatenate([acc[:, 128:], jnp.zeros((3 * CH, 112), F32)], axis=1)
    part[3 * CH:] = (tail[:CH] + pltpu.roll(tail[CH:2 * CH], 16, 1)
                     + pltpu.roll(tail[2 * CH:], 32, 1))

    def reduce_scatter(k):
        return remote(part.at[pl.ds(pl.multiple_of(pool_rank[k] * PART, 8), PART)],
                      got.at[0, k], as_sem.at[0, k], ar_sem.at[0, k], pool[k])

    def exchange(phase, k, to, spot):
        return remote(total.at[phase - 1], got.at[phase, spot], as_sem.at[phase, k], ar_sem.at[phase, k], to)

    def share(phase):
        seat = seats[phase]
        got[phase, seat] = total[phase - 1]
        for k in range(7):
            exchange(phase, k, (along_y, along_z)[phase - 1][k], seat).start()

    def gather(k):
        return remote(total.at[2], whole.at[here], as_sem.at[3, k], ar_sem.at[3, k], pool[k])

    def arrive(phase):
        for k in range(7):
            if phase == 0:
                reduce_scatter(k).wait_recv()
            else:
                to = (along_y, along_z)[phase - 1][k]
                exchange(phase, k, to, (seats[phase] + 7 - k) % 8).wait_recv()
        value = part[here] if phase == 0 else got[phase, 7]
        for k in range(7):
            value = value + got[phase, k]
        total[phase] = value

    here = pl.ds(pl.multiple_of(rank * PART, 8), PART)
    seats = [None, y, depth]
    corners_out = [
        remote(corner, cornerin.at[1], hs_sem.at[4], hr_sem.at[5], west),
        remote(corner, cornerin.at[0], hs_sem.at[5], hr_sem.at[4], east),
    ]
    for k in range(7):
        reduce_scatter(k).start()
    for copy in corners_out:
        copy.start()

    first = jnp.where(lane == 0, 1.0, 0.0)
    last = jnp.where(lane == ROWS - 1, 1.0, 0.0)
    north_f = is_north.astype(F32)
    south_f = is_south.astype(F32)

    def build_whole(ref, value, at, ring, down, up):
        rim = pltpu.roll(ring, (127 - 2 * at) % 128, 1)
        put(ref, at, 0, shifted_down(value) + rim * down)
        put(ref, at, 1, value)
        put(ref, at, 2, shifted_up(value) + rim * up)

    adj_down = first * (1.0 - north_f) + last * south_f
    adj_up = last * (1.0 - south_f) + first * north_f

    def product(ref, hi, lo, left, right):
        rhs = jnp.concatenate([ref[left], ref[right]], axis=1)
        rhs_hi, rhs_lo = rhs[:3 * CH], rhs[3 * CH:]
        out = dot_nn(hi, rhs_hi) + dot_nn(lo, rhs_hi) + dot_nn(hi, rhs_lo)
        p[left] = out[:, :ROWS]
        p[right] = out[:, ROWS:]

    def inner_build(ref, src, ring, down, up):
        def step(j, carry):
            build_whole(ref, column(src, j), j + 1, ring, down, up)
            return carry
        lax.fori_loop(0, COLS, step, 0)

    def inner_products(ref, hi, lo):
        def step(s, carry):
            product(ref, hi, lo, 2 * s + 1, 2 * s + 2)
            return carry
        lax.fori_loop(0, COLS // 2, step, 0)

    def finish(out_ref):
        def step(j, carry):
            out_ref[pl.ds(j, CH, stride=COLS), :] = (
                p[j, :CH] + p[j + 1, CH:2 * CH] + p[j + 2, 2 * CH:])
            return carry
        lax.fori_loop(0, COLS, step, 0)

    ring_g = pltpu.roll(beyond, 64, 1)
    inner_build(z, fv, beyond, first, last)
    inner_products(z, fwd_hi, fwd_lo)

    arrive(0)
    share(1)

    remote(corner, cornerin.at[1], hs_sem.at[4], hr_sem.at[5], west).wait_recv()
    remote(corner, cornerin.at[0], hs_sem.at[5], hr_sem.at[4], east).wait_recv()
    from_west, from_east = cornerin[0], cornerin[1]
    ends_f = jnp.where(lane < 2, pltpu.roll(from_west, 64, 1), pltpu.roll(from_east, 64, 1))
    ends_g = jnp.where(lane < 2, from_west, from_east)
    for at, side in ((0, 0), (COLS + 1, 1)):
        build_whole(z, colin[side, :CH], at, ends_f, first, last)
        build_whole(v, colin[side, CH:], at, ends_g, adj_down, adj_up)
    product(z, fwd_hi, fwd_lo, 0, COLS + 1)
    finish(resp_ref)
    inner_build(v, gv, ring_g, adj_down, adj_up)

    arrive(1)
    share(2)
    inner_products(v, adj_hi, adj_lo)
    product(v, adj_hi, adj_lo, 0, COLS + 1)
    finish(gfield_ref)

    arrive(2)
    for k in range(7):
        gather(k).start()
    whole[here] = total[2]
    for k in range(7):
        peer = pl.ds(pl.multiple_of((((x + 4 - near[k][0]) % 4) * 2 + (core + near[k][1]) % 2) * PART, 8), PART)
        remote(total.at[2], whole.at[peer], as_sem.at[3, k], ar_sem.at[3, k], pool[k]).wait_recv()
    rest = whole[3 * CH:]
    for b in range(3):
        rows = whole[b * CH:(b + 1) * CH] * scale
        extra = pltpu.roll(rest, (32 - 16 * b) % 128, 1) * scale
        gw_ref[b] = rows[:, :CH]
        gw_ref[3 + b] = pltpu.roll(rows, 80, 1)[:, :CH]
        gw_ref[6 + b] = jnp.where(lane < 32, pltpu.roll(rows, 32, 1), extra)[:, :CH]

    for copy in halo_out + corners_out:
        copy.wait_send()
    for k in range(7):
        reduce_scatter(k).wait_send()
        exchange(1, k, along_y[k], y).wait_send()
        exchange(2, k, along_z[k], depth).wait_send()
        gather(k).wait_send()


def body(state_field, weight_bank, cotangent):
    cells = CH * COLS
    total_cells = ROWS * lax.axis_size("lat") * COLS * lax.axis_size("lon")
    whole = pl.BlockSpec(memory_space=pltpu.VMEM)
    far = pl.BlockSpec(memory_space=pl.ANY)
    response, grad_field, grad_weight = pl.pallas_call(
        functools.partial(kernel, 1.0 / math.sqrt(total_cells)),
        out_shape=[
            jax.ShapeDtypeStruct((cells, ROWS), F32),
            jax.ShapeDtypeStruct((cells, ROWS), F32),
            jax.ShapeDtypeStruct((9, CH, CH), F32),
        ],
        in_specs=[far, far, whole],
        out_specs=[whole, whole, whole],
        scratch_shapes=[
            pltpu.VMEM((cells, ROWS), F32),
            pltpu.VMEM((cells, ROWS), F32),
            pltpu.VMEM((COLS + 2, 6 * CH, ROWS), BF16),
            pltpu.VMEM((COLS + 2, 6 * CH, ROWS), BF16),
            pltpu.VMEM((COLS + 2, 3 * CH, ROWS), F32),
            pltpu.VMEM((CH, ROWS), F32),
            pltpu.VMEM((2, CH, ROWS), F32),
            pltpu.VMEM((2, 2 * CH, ROWS), F32),
            pltpu.VMEM((2, 2 * CH, ROWS), F32),
            pltpu.VMEM((CH, ROWS), F32),
            pltpu.VMEM((2, CH, ROWS), F32),
            pltpu.VMEM((8 * PART, ROWS), F32),
            pltpu.VMEM((3, 8, PART, ROWS), F32),
            pltpu.VMEM((3, PART, ROWS), F32),
            pltpu.VMEM((8 * PART, ROWS), F32),
            pltpu.SemaphoreType.DMA((2,)),
            pltpu.SemaphoreType.DMA((6,)),
            pltpu.SemaphoreType.DMA((6,)),
            pltpu.SemaphoreType.DMA((4, 7)),
            pltpu.SemaphoreType.DMA((4, 7)),
        ],
        compiler_params=pltpu.CompilerParams(
            collective_id=0, has_side_effects=True, vmem_limit_bytes=40 << 20
        ),
        cost_estimate=pl.CostEstimate(
            flops=3 * 3 * 9 * CH * CH * COLS * ROWS * 2, bytes_accessed=16 * cells * ROWS, transcendentals=0
        ),
    )(state_field.reshape(cells, ROWS), cotangent.reshape(cells, ROWS), weight_bank)
    shape = (CH, COLS, ROWS)
    return response.reshape(shape), grad_field.reshape(shape), grad_weight


def solution(mesh):
    in_specs = (P(None, "lon", "lat"), P(), P(None, "lon", "lat"))
    out_specs = (P(None, "lon", "lat"), P(None, "lon", "lat"), P())
    return jax.shard_map(body, mesh=mesh, in_specs=in_specs, out_specs=out_specs, check_vma=False)
```

```python
import functools
import math

import jax
import jax.numpy as jnp
from jax import lax
from jax.experimental import pallas as pl
from jax.experimental.pallas import tpu as pltpu
from jax.sharding import PartitionSpec as P

CH = 48
COLS = 32
ROWS = 128
PART = 24
MESH = pl.DeviceIdType.MESH
F32 = jnp.float32
BF16 = jnp.bfloat16


def split(x):
    hi = x.astype(BF16)
    return hi, (x - hi.astype(F32)).astype(BF16)


def column(ref, j):
    return ref[pl.ds(j, CH, stride=COLS), :]


def dot_nn(a, b):
    return lax.dot_general(a, b, (((1,), (0,)), ((), ())), preferred_element_type=F32)


def dot_nt(a, b):
    return lax.dot_general(a, b, (((1,), (1,)), ((), ())), preferred_element_type=F32)


def remote(src, dst, send, recv, to):
    return pltpu.make_async_remote_copy(
        src_ref=src, dst_ref=dst, send_sem=send, recv_sem=recv,
        device_id=to, device_id_type=MESH,
    )


def kernel(f_hbm, g_hbm, w_hbm, resp, gfield, final,
           fv, gv, w_ref, z, v, p, q, edge, halo, colout, colin, corner, cornerin,
           part, got, total, whole, in_sem, hs_sem, hr_sem, as_sem, ar_sem):
    lon = lax.axis_index("lon")
    lat = lax.axis_index("lat")
    n_lon = lax.axis_size("lon")
    n_lat = lax.axis_size("lat")
    y, zh, core = lon // 8, (lon // 2) % 4, lon % 2
    x, zl = lat // 2, lat % 2
    depth = zh * 2 + zl
    is_north = jnp.where(lat == 0, 1, 0)
    is_south = jnp.where(lat == n_lat - 1, 1, 0)
    opposite = (lon + n_lon // 2) % n_lon

    def place(x, y, depth, core):
        return (y * 8 + (depth // 2) * 2 + core, x * 2 + depth % 2)

    west = ((lon + n_lon - 1) % n_lon, lat)
    east = ((lon + 1) % n_lon, lat)
    north = (jnp.where(lat == 0, opposite, lon), jnp.where(lat == 0, 0, lat - 1))
    south = (jnp.where(lat == n_lat - 1, opposite, lon),
             jnp.where(lat == n_lat - 1, n_lat - 1, lat + 1))
    near = [(dx, dc) for dx in range(4) for dc in range(2) if (dx, dc) != (0, 0)]
    pool = [place((x + dx) % 4, y, depth, (core + dc) % 2) for dx, dc in near]
    pool_rank = [((x + dx) % 4) * 2 + (core + dc) % 2 for dx, dc in near]
    along_y = [place(x, (y + k) % 8, depth, core) for k in range(1, 8)]
    along_z = [place(x, y, (depth + k) % 8, core) for k in range(1, 8)]
    rank = x * 2 + core

    barrier = pltpu.get_barrier_semaphore()
    partners = [west, east, north, south] + pool + along_y + along_z
    for to in partners:
        pl.semaphore_signal(barrier, inc=1, device_id=to, device_id_type=MESH)
    load_f = pltpu.make_async_copy(f_hbm, fv, in_sem.at[0])
    load_g = pltpu.make_async_copy(g_hbm, gv, in_sem.at[1])
    load_w = pltpu.make_async_copy(w_hbm, w_ref, in_sem.at[2])
    load_f.start()
    load_g.start()
    load_w.start()
    v[0] = jnp.zeros((6 * CH, ROWS), BF16)
    v[COLS + 1] = jnp.zeros((6 * CH, ROWS), BF16)
    load_f.wait()
    load_g.wait()

    lane = lax.broadcasted_iota(jnp.int32, (CH, ROWS), 1)

    def pack(j, acc):
        acc = jnp.where(lane // 2 == j, pltpu.roll(column(fv, j), 2 * j + 1, 1), acc)
        return jnp.where(lane // 2 == j + 32, pltpu.roll(column(gv, j), (2 * j + 65) % 128, 1), acc)

    edge[...] = lax.fori_loop(0, COLS, pack, jnp.zeros((CH, ROWS), F32), unroll=8)
    for side, j in enumerate((0, COLS - 1)):
        colout[side, :CH] = column(fv, j)
        colout[side, CH:] = column(gv, j)

    def put(ref, at, a, value):
        hi, lo = split(value)
        ref[at, a * CH:(a + 1) * CH] = hi
        ref[at, (3 + a) * CH:(4 + a) * CH] = lo

    def build(ref, at, value):
        put(ref, at, 0, jnp.where(lane == 0, 0.0, pltpu.roll(value, 1, 1)))
        put(ref, at, 1, value)
        put(ref, at, 2, jnp.where(lane == ROWS - 1, 0.0, pltpu.roll(value, ROWS - 1, 1)))

    def build_all(ref, src):
        def step(j, carry):
            build(ref, j + 1, column(src, j))
            return carry
        lax.fori_loop(0, COLS, step, 0, unroll=8)

    pl.semaphore_wait(barrier, len(partners))

    from_north = jnp.where(lat == 0, 0, 1)
    from_south = jnp.where(lat == n_lat - 1, 1, 0)
    halo_out = [
        remote(edge, halo.at[from_north], hs_sem.at[0], hr_sem.at[from_north], north),
        remote(edge, halo.at[from_south], hs_sem.at[1], hr_sem.at[from_south], south),
        remote(colout.at[0], colin.at[1], hs_sem.at[2], hr_sem.at[3], west),
        remote(colout.at[1], colin.at[0], hs_sem.at[3], hr_sem.at[2], east),
    ]
    for copy in halo_out:
        copy.start()

    build_all(z, fv)
    build_all(v, gv)

    def weight_step(lhs_hi, lhs_lo, rhs_hi, rhs_lo):
        return dot_nt(lhs_hi, rhs_hi) + dot_nt(lhs_lo, rhs_hi) + dot_nt(lhs_hi, rhs_lo)

    def local_weight(s, acc):
        sides = [[], [], [], []]
        for k in range(16):
            at = s * 16 + k + 1
            for low in range(2):
                r = (1 + 3 * low) * CH
                sides[low].append(jnp.concatenate(
                    [v[at + 1, r:r + CH], v[at, r:r + CH], v[at - 1, r:r + CH]], axis=0))
                sides[2 + low].append(z[at, 3 * CH * low:3 * CH * (low + 1)])
        return acc + weight_step(*[jnp.concatenate(s, axis=1) for s in sides])

    acc = lax.fori_loop(0, COLS // 16, local_weight, jnp.zeros((3 * CH, 3 * CH), F32))

    load_w.wait()
    forward = jnp.concatenate(
        [jnp.concatenate([w_ref[3 * a + b] for a in range(3)], axis=1) for b in range(3)], axis=0)
    turned = jnp.concatenate(
        [jnp.concatenate([w_ref[3 * (2 - a) + 2 - b] for b in range(3)], axis=1) for a in range(3)], axis=0)
    turned = jnp.concatenate([turned, jnp.zeros((3 * CH, 256 - 3 * CH), F32)], axis=1)
    turned = jnp.concatenate([turned, jnp.zeros((256 - 3 * CH, 256), F32)], axis=0)
    adjoint = turned.T[:3 * CH, :3 * CH]
    fwd_hi, fwd_lo = split(forward)
    adj_hi, adj_lo = split(adjoint)

    def product(out, ref, hi, lo, left, right):
        rhs = jnp.concatenate([ref[left], ref[right]], axis=1)
        rhs_hi, rhs_lo = rhs[:3 * CH], rhs[3 * CH:]
        value = dot_nn(hi, rhs_hi) + dot_nn(lo, rhs_hi) + dot_nn(hi, rhs_lo)
        out[left] = value[:, :ROWS]
        out[right] = value[:, ROWS:]

    def products(out, ref, hi, lo):
        def step(s, carry):
            product(out, ref, hi, lo, 2 * s + 1, 2 * s + 2)
            return carry
        lax.fori_loop(0, COLS // 2, step, 0, unroll=4)


    remote(colout.at[0], colin.at[1], hs_sem.at[2], hr_sem.at[3], west).wait_recv()
    remote(colout.at[1], colin.at[0], hs_sem.at[3], hr_sem.at[2], east).wait_recv()

    build(z, 0, colin[0, :CH])
    build(z, COLS + 1, colin[1, :CH])
    blank = jnp.zeros((CH, ROWS), BF16)
    outer = []
    for low in range(2):
        r = (1 + 3 * low) * CH
        outer.append(jnp.concatenate([
            jnp.concatenate([v[1, r:r + CH], blank], axis=1),
            jnp.concatenate([blank, blank], axis=1),
            jnp.concatenate([blank, v[COLS, r:r + CH]], axis=1)], axis=0))
    for low in range(2):
        r = 3 * CH * low
        outer.append(jnp.concatenate([z[0, r:r + 3 * CH], z[COLS + 1, r:r + 3 * CH]], axis=1))
    acc = acc + weight_step(*outer)

    def packed(value, left):
        hi = value.astype(BF16).astype(F32)
        lo = (value - hi).astype(BF16).astype(F32)
        first, second = (lo, hi) if left else (hi, lo)
        return jnp.concatenate([hi + pltpu.roll(first, 64, 1), second], axis=1).astype(BF16)

    own = edge[...]
    inside = lane < 64
    left_rows = []
    for b in (-1, 0, 1):
        value = pltpu.roll(own, (64 + 2 * b) % 128, 1)
        if b == 1:
            value = jnp.where(lane < 2, pltpu.roll(colin[0, CH:], 1, 1), value)
        if b == -1:
            value = jnp.where(lane >= 62, pltpu.roll(colin[1, CH:], 63, 1), value)
        left_rows.append(packed(jnp.where(inside, value, 0.0), True))
    remote(edge, halo.at[0], hs_sem.at[0], hr_sem.at[0], north).wait_recv()
    remote(edge, halo.at[1], hs_sem.at[1], hr_sem.at[1], south).wait_recv()
    beyond = jnp.where(
        lane % 2 == 0,
        pltpu.roll(halo[1], 1 + is_south, 1),
        pltpu.roll(halo[0], 3 - is_north, 1),
    )
    corner[...] = beyond
    across = pltpu.roll(beyond, 126, 1)
    right_rows = [
        packed(jnp.where(inside & (lane % 2 == 1), across, 0.0), False),
        jnp.zeros((CH, 256), BF16),
        packed(jnp.where(inside & (lane % 2 == 0), across, 0.0), False),
    ]
    acc = acc + dot_nt(jnp.concatenate(left_rows, axis=0), jnp.concatenate(right_rows, axis=0))

    part[:3 * CH] = acc[:, :128]
    tail = jnp.concatenate([acc[:, 128:], jnp.zeros((3 * CH, 112), F32)], axis=1)
    part[3 * CH:] = (tail[:CH] + pltpu.roll(tail[CH:2 * CH], 16, 1)
                     + pltpu.roll(tail[2 * CH:], 32, 1))

    def reduce_scatter(k):
        return remote(part.at[pl.ds(pl.multiple_of(pool_rank[k] * PART, 8), PART)],
                      got.at[0, k], as_sem.at[0, k], ar_sem.at[0, k], pool[k])

    def exchange(phase, k, to, spot):
        return remote(total.at[phase - 1], got.at[phase, spot], as_sem.at[phase, k], ar_sem.at[phase, k], to)

    def share(phase):
        seat = seats[phase]
        got[phase, seat] = total[phase - 1]
        for k in range(7):
            exchange(phase, k, (along_y, along_z)[phase - 1][k], seat).start()

    def gather(k):
        return remote(total.at[2], whole.at[here], as_sem.at[3, k], ar_sem.at[3, k], pool[k])

    def arrive(phase):
        for k in range(7):
            if phase == 0:
                reduce_scatter(k).wait_recv()
            else:
                to = (along_y, along_z)[phase - 1][k]
                exchange(phase, k, to, (seats[phase] + 7 - k) % 8).wait_recv()
        value = part[here] if phase == 0 else got[phase, 7]
        for k in range(7):
            value = value + got[phase, k]
        total[phase] = value

    here = pl.ds(pl.multiple_of(rank * PART, 8), PART)
    seats = [None, y, depth]
    corners_out = [
        remote(corner, cornerin.at[1], hs_sem.at[4], hr_sem.at[5], west),
        remote(corner, cornerin.at[0], hs_sem.at[5], hr_sem.at[4], east),
    ]
    for k in range(7):
        reduce_scatter(k).start()
    for copy in corners_out:
        copy.start()

    products(p, z, fwd_hi, fwd_lo)
    products(q, v, adj_hi, adj_lo)
    build(v, 0, colin[0, CH:])
    build(v, COLS + 1, colin[1, CH:])
    product(p, z, fwd_hi, fwd_lo, 0, COLS + 1)
    product(q, v, adj_hi, adj_lo, 0, COLS + 1)

    arrive(0)
    share(1)

    remote(corner, cornerin.at[1], hs_sem.at[4], hr_sem.at[5], west).wait_recv()
    remote(corner, cornerin.at[0], hs_sem.at[5], hr_sem.at[4], east).wait_recv()
    from_west, from_east = cornerin[0], cornerin[1]

    def finish(out, src, kernel_n, kernel_s, ring):
        weight_hi, weight_lo = split(jnp.concatenate([kernel_n, kernel_s], axis=1))
        odd = lane % 2 == 1
        ring_hi, ring_lo = split(jnp.concatenate(
            [jnp.where(odd, ring, 0.0), jnp.where(odd, 0.0, ring)], axis=0))
        terms = dot_nn(weight_hi, ring_hi) + dot_nn(weight_lo, ring_hi) + dot_nn(weight_hi, ring_lo)
        terms = (pltpu.roll(terms[:CH], 2, 1) + terms[CH:2 * CH]
                 + pltpu.roll(terms[2 * CH:], ROWS - 2, 1))
        rim = (lane == 0) | (lane == ROWS - 1)

        def step(j, carry):
            value = src[j, :CH] + src[j + 1, CH:2 * CH] + src[j + 2, 2 * CH:]
            value = value + jnp.where(rim, pltpu.roll(terms, 125 - 2 * j, 1), 0.0)
            out[pl.ds(j, CH, stride=COLS), :] = value
            return carry

        lax.fori_loop(0, COLS, step, 0, unroll=8)

    middle = (lane >= 2) & (lane < 66)
    ring_f = jnp.where(middle, beyond, jnp.where(
        lane < 2, pltpu.roll(from_west, 64, 1), pltpu.roll(from_east, 64, 1)))
    finish(resp, p, forward[:, :CH], forward[:, 2 * CH:], ring_f)

    arrive(1)
    share(2)
    low_side, high_side = adjoint[:, :CH], adjoint[:, 2 * CH:]
    ring_g = jnp.where(middle, pltpu.roll(beyond, 64, 1), jnp.where(lane < 2, from_west, from_east))
    finish(gfield, q, jnp.where(lat == 0, high_side, low_side),
           jnp.where(lat == n_lat - 1, low_side, high_side), ring_g)

    arrive(2)
    for k in range(7):
        gather(k).start()
    whole[here] = total[2]
    for k in range(7):
        peer = pl.ds(pl.multiple_of((((x + 4 - near[k][0]) % 4) * 2 + (core + near[k][1]) % 2) * PART, 8), PART)
        remote(total.at[2], whole.at[peer], as_sem.at[3, k], ar_sem.at[3, k], pool[k]).wait_recv()
    final[...] = whole[...]
    for copy in halo_out + corners_out:
        copy.wait_send()
    for k in range(7):
        reduce_scatter(k).wait_send()
        exchange(1, k, along_y[k], y).wait_send()
        exchange(2, k, along_z[k], depth).wait_send()
        gather(k).wait_send()


def hand_over(scale, resp, gfield, final, resp_hbm, gfield_hbm, gw_hbm, gw, sem):
    stores = [
        pltpu.make_async_copy(resp, resp_hbm, sem.at[0]),
        pltpu.make_async_copy(gfield, gfield_hbm, sem.at[1]),
        pltpu.make_async_copy(gw, gw_hbm, sem.at[2]),
    ]
    stores[0].start()
    stores[1].start()
    lane = lax.broadcasted_iota(jnp.int32, (CH, ROWS), 1)
    rest = final[3 * CH:]
    for b in range(3):
        rows = final[b * CH:(b + 1) * CH] * scale
        extra = pltpu.roll(rest, (32 - 16 * b) % 128, 1) * scale
        gw[b] = rows[:, :CH]
        gw[3 + b] = pltpu.roll(rows, 80, 1)[:, :CH]
        gw[6 + b] = jnp.where(lane < 32, pltpu.roll(rows, 32, 1), extra)[:, :CH]
    stores[2].start()
    for copy in stores:
        copy.wait()


def body(state_field, weight_bank, cotangent):
    cells = CH * COLS
    total_cells = ROWS * lax.axis_size("lat") * COLS * lax.axis_size("lon")
    near = pl.BlockSpec(memory_space=pltpu.VMEM)
    far = pl.BlockSpec(memory_space=pltpu.HBM)
    field = jax.ShapeDtypeStruct((cells, ROWS), F32)
    held = lambda *dims: pltpu.VMEM(dims, F32)
    pinned = lambda value: pltpu.with_memory_space_constraint(value, pltpu.HBM)
    parts = pl.pallas_call(
        kernel,
        out_shape=[held(cells, ROWS), held(cells, ROWS), held(8 * PART, ROWS)],
        in_specs=[far, far, far],
        out_specs=[near, near, near],
        scratch_shapes=[
            pltpu.VMEM((cells, ROWS), F32),
            pltpu.VMEM((cells, ROWS), F32),
            pltpu.VMEM((9, CH, CH), F32),
            pltpu.VMEM((COLS + 2, 6 * CH, ROWS), BF16),
            pltpu.VMEM((COLS + 2, 6 * CH, ROWS), BF16),
            pltpu.VMEM((COLS + 2, 3 * CH, ROWS), F32),
            pltpu.VMEM((COLS + 2, 3 * CH, ROWS), F32),
            pltpu.VMEM((CH, ROWS), F32),
            pltpu.VMEM((2, CH, ROWS), F32),
            pltpu.VMEM((2, 2 * CH, ROWS), F32),
            pltpu.VMEM((2, 2 * CH, ROWS), F32),
            pltpu.VMEM((CH, ROWS), F32),
            pltpu.VMEM((2, CH, ROWS), F32),
            pltpu.VMEM((8 * PART, ROWS), F32),
            pltpu.VMEM((3, 8, PART, ROWS), F32),
            pltpu.VMEM((3, PART, ROWS), F32),
            pltpu.VMEM((8 * PART, ROWS), F32),
            pltpu.SemaphoreType.DMA((3,)),
            pltpu.SemaphoreType.DMA((6,)),
            pltpu.SemaphoreType.DMA((6,)),
            pltpu.SemaphoreType.DMA((4, 7)),
            pltpu.SemaphoreType.DMA((4, 7)),
        ],
        compiler_params=pltpu.CompilerParams(
            collective_id=0, has_side_effects=True, vmem_limit_bytes=40 << 20
        ),
        cost_estimate=pl.CostEstimate(
            flops=3 * 3 * 9 * CH * CH * COLS * ROWS * 2, bytes_accessed=16 * cells * ROWS, transcendentals=0
        ),
    )(pinned(state_field.reshape(cells, ROWS)), pinned(cotangent.reshape(cells, ROWS)), pinned(weight_bank))
    response, grad_field, grad_weight = pl.pallas_call(
        functools.partial(hand_over, 1.0 / math.sqrt(total_cells)),
        out_shape=[field, field, jax.ShapeDtypeStruct((9, CH, CH), F32)],
        in_specs=[near, near, near],
        out_specs=[far, far, far],
        scratch_shapes=[pltpu.VMEM((9, CH, CH), F32), pltpu.SemaphoreType.DMA((3,))],
    )(*[pltpu.with_memory_space_constraint(value, pltpu.VMEM) for value in parts])
    shape = (CH, COLS, ROWS)
    return response.reshape(shape), grad_field.reshape(shape), grad_weight


def solution(mesh):
    in_specs = (P(None, "lon", "lat"), P(), P(None, "lon", "lat"))
    out_specs = (P(None, "lon", "lat"), P(None, "lon", "lat"), P())
    return jax.shard_map(body, mesh=mesh, in_specs=in_specs, out_specs=out_specs, check_vma=False)
```

```python
import functools
import math

import jax
import jax.numpy as jnp
from jax import lax
from jax.experimental import pallas as pl
from jax.experimental.pallas import tpu as pltpu
from jax.sharding import PartitionSpec as P

CH = 48
COLS = 32
ROWS = 128
PART = 24
THICK = 16
MESH = pl.DeviceIdType.MESH
F32 = jnp.float32
BF16 = jnp.bfloat16


def split(x):
    hi = x.astype(BF16)
    return hi, (x - hi.astype(F32)).astype(BF16)


def column(ref, j):
    return ref[pl.ds(j, CH, stride=COLS), :]


def dot_nn(a, b):
    return lax.dot_general(a, b, (((1,), (0,)), ((), ())), preferred_element_type=F32)


def dot_nt(a, b):
    return lax.dot_general(a, b, (((1,), (1,)), ((), ())), preferred_element_type=F32)


def remote(src, dst, send, recv, to):
    return pltpu.make_async_remote_copy(
        src_ref=src, dst_ref=dst, send_sem=send, recv_sem=recv,
        device_id=to, device_id_type=MESH,
    )


def kernel(f_hbm, g_hbm, w_hbm, resp, gfield, final,
           fv, gv, w_ref, z, v, p, q, edge, halo, colout, colin, corner, cornerin,
           part, pooled, thick, thin, whole, in_sem, hs_sem, hr_sem, as_sem, ar_sem):
    lon = lax.axis_index("lon")
    lat = lax.axis_index("lat")
    n_lon = lax.axis_size("lon")
    n_lat = lax.axis_size("lat")
    y, zh, core = lon // 8, (lon // 2) % 4, lon % 2
    x, zl = lat // 2, lat % 2
    depth = zh * 2 + zl
    is_north = jnp.where(lat == 0, 1, 0)
    is_south = jnp.where(lat == n_lat - 1, 1, 0)
    opposite = (lon + n_lon // 2) % n_lon

    def place(x, y, depth, core):
        return (y * 8 + (depth // 2) * 2 + core, x * 2 + depth % 2)

    west = ((lon + n_lon - 1) % n_lon, lat)
    east = ((lon + 1) % n_lon, lat)
    north = (jnp.where(lat == 0, opposite, lon), jnp.where(lat == 0, 0, lat - 1))
    south = (jnp.where(lat == n_lat - 1, opposite, lon),
             jnp.where(lat == n_lat - 1, n_lat - 1, lat + 1))
    rank = x * 2 + core

    def others(own):
        return [k + jnp.where(own <= k, 1, 0) for k in range(7)]

    first_is_y = core == 0
    seats = (jnp.where(first_is_y, y, depth), jnp.where(first_is_y, depth, y))

    def along(way, seat):
        by_y = first_is_y if way == 0 else jnp.logical_not(first_is_y)
        return place(x, jnp.where(by_y, seat, y), jnp.where(by_y, depth, seat), core)

    def pool(seat):
        return place(seat // 2, y, depth, seat % 2)

    barrier = pltpu.get_barrier_semaphore()
    partners = [west, east, north, south] + [pool(k) for k in others(rank)]
    partners += [along(way, k) for way in range(2) for k in others(seats[way])]
    for to in partners:
        pl.semaphore_signal(barrier, inc=1, device_id=to, device_id_type=MESH)
    load_f = pltpu.make_async_copy(f_hbm, fv, in_sem.at[0])
    load_g = pltpu.make_async_copy(g_hbm, gv, in_sem.at[1])
    load_w = pltpu.make_async_copy(w_hbm, w_ref, in_sem.at[2])
    load_f.start()
    load_g.start()
    load_w.start()
    v[0] = jnp.zeros((6 * CH, ROWS), BF16)
    v[COLS + 1] = jnp.zeros((6 * CH, ROWS), BF16)
    load_f.wait()
    load_g.wait()

    lane = lax.broadcasted_iota(jnp.int32, (CH, ROWS), 1)

    def pack(j, acc):
        acc = jnp.where(lane // 2 == j, pltpu.roll(column(fv, j), 2 * j + 1, 1), acc)
        return jnp.where(lane // 2 == j + 32, pltpu.roll(column(gv, j), (2 * j + 65) % 128, 1), acc)

    edge[...] = lax.fori_loop(0, COLS, pack, jnp.zeros((CH, ROWS), F32), unroll=8)
    for side, j in enumerate((0, COLS - 1)):
        colout[side, :CH] = column(fv, j)
        colout[side, CH:] = column(gv, j)

    def put(ref, at, a, value):
        hi, lo = split(value)
        ref[at, a * CH:(a + 1) * CH] = hi
        ref[at, (3 + a) * CH:(4 + a) * CH] = lo

    def build(ref, at, value):
        put(ref, at, 0, jnp.where(lane == 0, 0.0, pltpu.roll(value, 1, 1)))
        put(ref, at, 1, value)
        put(ref, at, 2, jnp.where(lane == ROWS - 1, 0.0, pltpu.roll(value, ROWS - 1, 1)))

    def build_all(ref, src):
        def step(j, carry):
            build(ref, j + 1, column(src, j))
            return carry
        lax.fori_loop(0, COLS, step, 0, unroll=8)

    pl.semaphore_wait(barrier, len(partners))

    from_north = jnp.where(lat == 0, 0, 1)
    from_south = jnp.where(lat == n_lat - 1, 1, 0)
    halo_out = [
        remote(edge, halo.at[from_north], hs_sem.at[0], hr_sem.at[from_north], north),
        remote(edge, halo.at[from_south], hs_sem.at[1], hr_sem.at[from_south], south),
        remote(colout.at[0], colin.at[1], hs_sem.at[2], hr_sem.at[3], west),
        remote(colout.at[1], colin.at[0], hs_sem.at[3], hr_sem.at[2], east),
    ]
    for copy in halo_out:
        copy.start()

    build_all(z, fv)
    build_all(v, gv)

    def weight_step(lhs_hi, lhs_lo, rhs_hi, rhs_lo):
        return dot_nt(lhs_hi, rhs_hi) + dot_nt(lhs_lo, rhs_hi) + dot_nt(lhs_hi, rhs_lo)

    def local_weight(s, acc):
        sides = [[], [], [], []]
        for k in range(16):
            at = s * 16 + k + 1
            for low in range(2):
                r = (1 + 3 * low) * CH
                sides[low].append(jnp.concatenate(
                    [v[at + 1, r:r + CH], v[at, r:r + CH], v[at - 1, r:r + CH]], axis=0))
                sides[2 + low].append(z[at, 3 * CH * low:3 * CH * (low + 1)])
        return acc + weight_step(*[jnp.concatenate(s, axis=1) for s in sides])

    acc = lax.fori_loop(0, COLS // 16, local_weight, jnp.zeros((3 * CH, 3 * CH), F32))

    load_w.wait()
    forward = jnp.concatenate(
        [jnp.concatenate([w_ref[3 * a + b] for a in range(3)], axis=1) for b in range(3)], axis=0)
    turned = jnp.concatenate(
        [jnp.concatenate([w_ref[3 * (2 - a) + 2 - b] for b in range(3)], axis=1) for a in range(3)], axis=0)
    turned = jnp.concatenate([turned, jnp.zeros((3 * CH, 256 - 3 * CH), F32)], axis=1)
    turned = jnp.concatenate([turned, jnp.zeros((256 - 3 * CH, 256), F32)], axis=0)
    adjoint = turned.T[:3 * CH, :3 * CH]
    fwd_hi, fwd_lo = split(forward)
    adj_hi, adj_lo = split(adjoint)

    def product(out, ref, hi, lo, left, right):
        rhs = jnp.concatenate([ref[left], ref[right]], axis=1)
        rhs_hi, rhs_lo = rhs[:3 * CH], rhs[3 * CH:]
        value = dot_nn(hi, rhs_hi) + dot_nn(lo, rhs_hi) + dot_nn(hi, rhs_lo)
        out[left] = value[:, :ROWS]
        out[right] = value[:, ROWS:]

    def products(out, ref, hi, lo):
        def step(s, carry):
            product(out, ref, hi, lo, 2 * s + 1, 2 * s + 2)
            return carry
        lax.fori_loop(0, COLS // 2, step, 0, unroll=4)


    remote(colout.at[0], colin.at[1], hs_sem.at[2], hr_sem.at[3], west).wait_recv()
    remote(colout.at[1], colin.at[0], hs_sem.at[3], hr_sem.at[2], east).wait_recv()

    build(z, 0, colin[0, :CH])
    build(z, COLS + 1, colin[1, :CH])
    blank = jnp.zeros((CH, ROWS), BF16)
    outer = []
    for low in range(2):
        r = (1 + 3 * low) * CH
        outer.append(jnp.concatenate([
            jnp.concatenate([v[1, r:r + CH], blank], axis=1),
            jnp.concatenate([blank, blank], axis=1),
            jnp.concatenate([blank, v[COLS, r:r + CH]], axis=1)], axis=0))
    for low in range(2):
        r = 3 * CH * low
        outer.append(jnp.concatenate([z[0, r:r + 3 * CH], z[COLS + 1, r:r + 3 * CH]], axis=1))
    acc = acc + weight_step(*outer)

    def packed(value, left):
        hi = value.astype(BF16).astype(F32)
        lo = (value - hi).astype(BF16).astype(F32)
        first, second = (lo, hi) if left else (hi, lo)
        return jnp.concatenate([hi + pltpu.roll(first, 64, 1), second], axis=1).astype(BF16)

    own = edge[...]
    inside = lane < 64
    left_rows = []
    for b in (-1, 0, 1):
        value = pltpu.roll(own, (64 + 2 * b) % 128, 1)
        if b == 1:
            value = jnp.where(lane < 2, pltpu.roll(colin[0, CH:], 1, 1), value)
        if b == -1:
            value = jnp.where(lane >= 62, pltpu.roll(colin[1, CH:], 63, 1), value)
        left_rows.append(packed(jnp.where(inside, value, 0.0), True))
    remote(edge, halo.at[0], hs_sem.at[0], hr_sem.at[0], north).wait_recv()
    remote(edge, halo.at[1], hs_sem.at[1], hr_sem.at[1], south).wait_recv()
    beyond = jnp.where(
        lane % 2 == 0,
        pltpu.roll(halo[1], 1 + is_south, 1),
        pltpu.roll(halo[0], 3 - is_north, 1),
    )
    corner[...] = beyond
    across = pltpu.roll(beyond, 126, 1)
    right_rows = [
        packed(jnp.where(inside & (lane % 2 == 1), across, 0.0), False),
        jnp.zeros((CH, 256), BF16),
        packed(jnp.where(inside & (lane % 2 == 0), across, 0.0), False),
    ]
    acc = acc + dot_nt(jnp.concatenate(left_rows, axis=0), jnp.concatenate(right_rows, axis=0))

    part[:3 * CH] = acc[:, :128]
    tail = jnp.concatenate([acc[:, 128:], jnp.zeros((3 * CH, 112), F32)], axis=1)
    part[3 * CH:] = (tail[:CH] + pltpu.roll(tail[CH:2 * CH], 16, 1)
                     + pltpu.roll(tail[2 * CH:], 32, 1))

    def chunk(seat):
        return pl.ds(pl.multiple_of(seat * PART, 8), PART)

    def scatter(to):
        return remote(part.at[chunk(to)], pooled.at[rank], as_sem.at[0, to], ar_sem.at[0, rank], pool(to))

    def exchange(slots, stage, way, to):
        own = slots.at[stage - 1, seats[way]]
        line = 2 * stage - 1 if slots is thick else 2 * stage
        return remote(own, own, as_sem.at[line, to], ar_sem.at[line, seats[way]], along(way, to))

    def exchanged(slots, stage, way, by):
        line = 2 * stage - 1 if slots is thick else 2 * stage
        spot = slots.at[stage - 1, by]
        return remote(spot, spot, as_sem.at[line, by], ar_sem.at[line, by], along(way, by))

    def gather(to):
        return remote(whole.at[chunk(rank)], whole.at[chunk(rank)], as_sem.at[5, to], ar_sem.at[5, rank], pool(to))

    def total(slots):
        value = slots[0]
        for k in range(1, 8):
            value = value + slots[k]
        return value

    def share(stage, thick_value, thin_value):
        ways = (0, 1) if stage == 1 else (1, 0)
        thick[stage - 1, seats[ways[0]]] = thick_value
        thin[stage - 1, seats[ways[1]]] = thin_value
        for slots, way in zip((thick, thin), ways):
            for to in others(seats[way]):
                exchange(slots, stage, way, to).start()

    def collect(stage):
        ways = (0, 1) if stage == 1 else (1, 0)
        for slots, way in zip((thick, thin), ways):
            for by in others(seats[way]):
                exchanged(slots, stage, way, by).wait_recv()
        return total(thick.at[stage - 1]), total(thin.at[stage - 1])

    corners_out = [
        remote(corner, cornerin.at[1], hs_sem.at[4], hr_sem.at[5], west),
        remote(corner, cornerin.at[0], hs_sem.at[5], hr_sem.at[4], east),
    ]
    for to in others(rank):
        scatter(to).start()
    pooled[rank] = part[chunk(rank)]
    for copy in corners_out:
        copy.start()

    products(p, z, fwd_hi, fwd_lo)
    product(p, z, fwd_hi, fwd_lo, 0, COLS + 1)

    for by in others(rank):
        remote(pooled.at[by], pooled.at[by], as_sem.at[0, by], ar_sem.at[0, by], pool(by)).wait_recv()
    sums = total(pooled)
    share(1, sums[:THICK], sums[THICK:])

    build(v, 0, colin[0, CH:])
    build(v, COLS + 1, colin[1, CH:])
    products(q, v, adj_hi, adj_lo)
    product(q, v, adj_hi, adj_lo, 0, COLS + 1)

    remote(corner, cornerin.at[1], hs_sem.at[4], hr_sem.at[5], west).wait_recv()
    remote(corner, cornerin.at[0], hs_sem.at[5], hr_sem.at[4], east).wait_recv()
    from_west, from_east = cornerin[0], cornerin[1]

    def finish(out, src, kernel_n, kernel_s, ring):
        weight_hi, weight_lo = split(jnp.concatenate([kernel_n, kernel_s], axis=1))
        odd = lane % 2 == 1
        ring_hi, ring_lo = split(jnp.concatenate(
            [jnp.where(odd, ring, 0.0), jnp.where(odd, 0.0, ring)], axis=0))
        terms = dot_nn(weight_hi, ring_hi) + dot_nn(weight_lo, ring_hi) + dot_nn(weight_hi, ring_lo)
        terms = (pltpu.roll(terms[:CH], 2, 1) + terms[CH:2 * CH]
                 + pltpu.roll(terms[2 * CH:], ROWS - 2, 1))
        rim = (lane == 0) | (lane == ROWS - 1)

        def step(j, carry):
            value = src[j, :CH] + src[j + 1, CH:2 * CH] + src[j + 2, 2 * CH:]
            value = value + jnp.where(rim, pltpu.roll(terms, 125 - 2 * j, 1), 0.0)
            out[pl.ds(j, CH, stride=COLS), :] = value
            return carry

        lax.fori_loop(0, COLS, step, 0, unroll=8)

    middle = (lane >= 2) & (lane < 66)
    ring_f = jnp.where(middle, beyond, jnp.where(
        lane < 2, pltpu.roll(from_west, 64, 1), pltpu.roll(from_east, 64, 1)))
    finish(resp, p, forward[:, :CH], forward[:, 2 * CH:], ring_f)

    share(2, *collect(1))

    low_side, high_side = adjoint[:, :CH], adjoint[:, 2 * CH:]
    ring_g = jnp.where(middle, pltpu.roll(beyond, 64, 1), jnp.where(lane < 2, from_west, from_east))
    finish(gfield, q, jnp.where(lat == 0, high_side, low_side),
           jnp.where(lat == n_lat - 1, low_side, high_side), ring_g)

    whole[chunk(rank)] = jnp.concatenate(collect(2), axis=0)
    for to in others(rank):
        gather(to).start()
    for by in others(rank):
        remote(whole.at[chunk(by)], whole.at[chunk(by)], as_sem.at[5, by], ar_sem.at[5, by], pool(by)).wait_recv()
    final[...] = whole[...]
    for copy in halo_out + corners_out:
        copy.wait_send()
    for to in others(rank):
        scatter(to).wait_send()
        gather(to).wait_send()
    for stage in (1, 2):
        ways = (0, 1) if stage == 1 else (1, 0)
        for slots, way in zip((thick, thin), ways):
            for to in others(seats[way]):
                exchange(slots, stage, way, to).wait_send()


def hand_over(scale, resp, gfield, final, resp_hbm, gfield_hbm, gw_hbm, gw, sem):
    stores = [
        pltpu.make_async_copy(resp, resp_hbm, sem.at[0]),
        pltpu.make_async_copy(gfield, gfield_hbm, sem.at[1]),
        pltpu.make_async_copy(gw, gw_hbm, sem.at[2]),
    ]
    stores[0].start()
    stores[1].start()
    lane = lax.broadcasted_iota(jnp.int32, (CH, ROWS), 1)
    rest = final[3 * CH:]
    for b in range(3):
        rows = final[b * CH:(b + 1) * CH] * scale
        extra = pltpu.roll(rest, (32 - 16 * b) % 128, 1) * scale
        gw[b] = rows[:, :CH]
        gw[3 + b] = pltpu.roll(rows, 80, 1)[:, :CH]
        gw[6 + b] = jnp.where(lane < 32, pltpu.roll(rows, 32, 1), extra)[:, :CH]
    stores[2].start()
    for copy in stores:
        copy.wait()


def body(state_field, weight_bank, cotangent):
    cells = CH * COLS
    total_cells = ROWS * lax.axis_size("lat") * COLS * lax.axis_size("lon")
    near = pl.BlockSpec(memory_space=pltpu.VMEM)
    far = pl.BlockSpec(memory_space=pltpu.HBM)
    field = jax.ShapeDtypeStruct((cells, ROWS), F32)
    held = lambda *dims: pltpu.VMEM(dims, F32)
    pinned = lambda value: pltpu.with_memory_space_constraint(value, pltpu.HBM)
    parts = pl.pallas_call(
        kernel,
        out_shape=[held(cells, ROWS), held(cells, ROWS), held(8 * PART, ROWS)],
        in_specs=[far, far, far],
        out_specs=[near, near, near],
        scratch_shapes=[
            pltpu.VMEM((cells, ROWS), F32),
            pltpu.VMEM((cells, ROWS), F32),
            pltpu.VMEM((9, CH, CH), F32),
            pltpu.VMEM((COLS + 2, 6 * CH, ROWS), BF16),
            pltpu.VMEM((COLS + 2, 6 * CH, ROWS), BF16),
            pltpu.VMEM((COLS + 2, 3 * CH, ROWS), F32),
            pltpu.VMEM((COLS + 2, 3 * CH, ROWS), F32),
            pltpu.VMEM((CH, ROWS), F32),
            pltpu.VMEM((2, CH, ROWS), F32),
            pltpu.VMEM((2, 2 * CH, ROWS), F32),
            pltpu.VMEM((2, 2 * CH, ROWS), F32),
            pltpu.VMEM((CH, ROWS), F32),
            pltpu.VMEM((2, CH, ROWS), F32),
            pltpu.VMEM((8 * PART, ROWS), F32),
            pltpu.VMEM((8, PART, ROWS), F32),
            pltpu.VMEM((2, 8, THICK, ROWS), F32),
            pltpu.VMEM((2, 8, PART - THICK, ROWS), F32),
            pltpu.VMEM((8 * PART, ROWS), F32),
            pltpu.SemaphoreType.DMA((3,)),
            pltpu.SemaphoreType.DMA((6,)),
            pltpu.SemaphoreType.DMA((6,)),
            pltpu.SemaphoreType.DMA((6, 8)),
            pltpu.SemaphoreType.DMA((6, 8)),
        ],
        compiler_params=pltpu.CompilerParams(
            collective_id=0, has_side_effects=True, vmem_limit_bytes=40 << 20
        ),
        cost_estimate=pl.CostEstimate(
            flops=3 * 3 * 9 * CH * CH * COLS * ROWS * 2, bytes_accessed=16 * cells * ROWS, transcendentals=0
        ),
    )(pinned(state_field.reshape(cells, ROWS)), pinned(cotangent.reshape(cells, ROWS)), pinned(weight_bank))
    response, grad_field, grad_weight = pl.pallas_call(
        functools.partial(hand_over, 1.0 / math.sqrt(total_cells)),
        out_shape=[field, field, jax.ShapeDtypeStruct((9, CH, CH), F32)],
        in_specs=[near, near, near],
        out_specs=[far, far, far],
        scratch_shapes=[pltpu.VMEM((9, CH, CH), F32), pltpu.SemaphoreType.DMA((3,))],
    )(*[pltpu.with_memory_space_constraint(value, pltpu.VMEM) for value in parts])
    shape = (CH, COLS, ROWS)
    return response.reshape(shape), grad_field.reshape(shape), grad_weight


def solution(mesh):
    in_specs = (P(None, "lon", "lat"), P(), P(None, "lon", "lat"))
    out_specs = (P(None, "lon", "lat"), P(None, "lon", "lat"), P())
    return jax.shard_map(body, mesh=mesh, in_specs=in_specs, out_specs=out_specs, check_vma=False)
```

```python
import functools
import math

import jax
import jax.numpy as jnp
from jax import lax
from jax.experimental import pallas as pl
from jax.experimental.pallas import tpu as pltpu
from jax.sharding import PartitionSpec as P

CH = 48
COLS = 32
ROWS = 128
PART = 24
THICK = 16
MESH = pl.DeviceIdType.MESH
F32 = jnp.float32
BF16 = jnp.bfloat16


def split(x):
    hi = x.astype(BF16)
    return hi, (x - hi.astype(F32)).astype(BF16)


def column(ref, j):
    return ref[pl.ds(j, CH, stride=COLS), :]


def dot_nn(a, b):
    return lax.dot_general(a, b, (((1,), (0,)), ((), ())), preferred_element_type=F32)


def dot_nt(a, b):
    return lax.dot_general(a, b, (((1,), (1,)), ((), ())), preferred_element_type=F32)


def remote(src, dst, send, recv, to):
    return pltpu.make_async_remote_copy(
        src_ref=src, dst_ref=dst, send_sem=send, recv_sem=recv,
        device_id=to, device_id_type=MESH,
    )


def kernel(f_hbm, g_hbm, w_hbm, resp, gfield, final,
           fv, gv, w_ref, z, v, p, q, edge, halo, colout, colin, corner, cornerin,
           part, pooled, thick, thin, whole, in_sem, hs_sem, hr_sem, as_sem, ar_sem):
    lon = lax.axis_index("lon")
    lat = lax.axis_index("lat")
    n_lon = lax.axis_size("lon")
    n_lat = lax.axis_size("lat")
    y, zh, core = lon // 8, (lon // 2) % 4, lon % 2
    x, zl = lat // 2, lat % 2
    depth = zh * 2 + zl
    is_north = jnp.where(lat == 0, 1, 0)
    is_south = jnp.where(lat == n_lat - 1, 1, 0)
    opposite = (lon + n_lon // 2) % n_lon

    def place(x, y, depth, core):
        return (y * 8 + (depth // 2) * 2 + core, x * 2 + depth % 2)

    west = ((lon + n_lon - 1) % n_lon, lat)
    east = ((lon + 1) % n_lon, lat)
    north = (jnp.where(lat == 0, opposite, lon), jnp.where(lat == 0, 0, lat - 1))
    south = (jnp.where(lat == n_lat - 1, opposite, lon),
             jnp.where(lat == n_lat - 1, n_lat - 1, lat + 1))
    rank = x * 2 + core

    def others(own):
        return [k + jnp.where(own <= k, 1, 0) for k in range(7)]

    first_is_y = core == 0
    seats = (jnp.where(first_is_y, y, depth), jnp.where(first_is_y, depth, y))

    def along(way, seat):
        by_y = first_is_y if way == 0 else jnp.logical_not(first_is_y)
        return place(x, jnp.where(by_y, seat, y), jnp.where(by_y, depth, seat), core)

    def pool(seat):
        return place(seat // 2, y, depth, seat % 2)

    barrier = pltpu.get_barrier_semaphore()
    partners = [west, east, north, south] + [pool(k) for k in others(rank)]
    partners += [along(way, k) for way in range(2) for k in others(seats[way])]
    load_f = pltpu.make_async_copy(f_hbm, fv, in_sem.at[0])
    load_g = pltpu.make_async_copy(g_hbm, gv, in_sem.at[1])
    load_w = pltpu.make_async_copy(w_hbm, w_ref, in_sem.at[2])
    load_f.start()
    load_g.start()
    load_w.start()
    for to in partners:
        pl.semaphore_signal(barrier, inc=1, device_id=to, device_id_type=MESH)
    v[0] = jnp.zeros((6 * CH, ROWS), BF16)
    v[COLS + 1] = jnp.zeros((6 * CH, ROWS), BF16)
    lane = lax.broadcasted_iota(jnp.int32, (CH, ROWS), 1)

    def pack(src, base, acc):
        def step(j, acc):
            return jnp.where(lane // 2 == j + base // 2, pltpu.roll(column(src, j), (2 * j + base + 1) % 128, 1), acc)
        return lax.fori_loop(0, COLS, step, acc, unroll=16)

    load_f.wait()
    packed_f = pack(fv, 0, jnp.zeros((CH, ROWS), F32))
    load_g.wait()
    edge[...] = pack(gv, 64, packed_f)
    for side, j in enumerate((0, COLS - 1)):
        colout[side, :CH] = column(fv, j)
        colout[side, CH:] = column(gv, j)

    def put(ref, at, a, value):
        hi, lo = split(value)
        ref[at, a * CH:(a + 1) * CH] = hi
        ref[at, (3 + a) * CH:(4 + a) * CH] = lo

    def build(ref, at, value):
        put(ref, at, 0, jnp.where(lane == 0, 0.0, pltpu.roll(value, 1, 1)))
        put(ref, at, 1, value)
        put(ref, at, 2, jnp.where(lane == ROWS - 1, 0.0, pltpu.roll(value, ROWS - 1, 1)))

    def build_all(ref, src):
        def step(j, carry):
            build(ref, j + 1, column(src, j))
            return carry
        lax.fori_loop(0, COLS, step, 0, unroll=8)

    pl.semaphore_wait(barrier, len(partners))

    from_north = jnp.where(lat == 0, 0, 1)
    from_south = jnp.where(lat == n_lat - 1, 1, 0)
    halo_out = [
        remote(colout.at[0], colin.at[1], hs_sem.at[2], hr_sem.at[3], west),
        remote(colout.at[1], colin.at[0], hs_sem.at[3], hr_sem.at[2], east),
        remote(edge, halo.at[from_north], hs_sem.at[0], hr_sem.at[from_north], north),
        remote(edge, halo.at[from_south], hs_sem.at[1], hr_sem.at[from_south], south),
    ]
    for copy in halo_out:
        copy.start()

    build_all(z, fv)
    build_all(v, gv)

    def weight_step(lhs_hi, lhs_lo, rhs_hi, rhs_lo):
        return dot_nt(lhs_hi, rhs_hi) + dot_nt(lhs_lo, rhs_hi) + dot_nt(lhs_hi, rhs_lo)

    def local_weight(s, acc):
        sides = [[], [], [], []]
        for k in range(16):
            at = s * 16 + k + 1
            for low in range(2):
                r = (1 + 3 * low) * CH
                sides[low].append(jnp.concatenate(
                    [v[at + 1, r:r + CH], v[at, r:r + CH], v[at - 1, r:r + CH]], axis=0))
                sides[2 + low].append(z[at, 3 * CH * low:3 * CH * (low + 1)])
        return acc + weight_step(*[jnp.concatenate(s, axis=1) for s in sides])

    acc = lax.fori_loop(0, COLS // 16, local_weight, jnp.zeros((3 * CH, 3 * CH), F32))

    load_w.wait()
    forward = jnp.concatenate(
        [jnp.concatenate([w_ref[3 * a + b] for a in range(3)], axis=1) for b in range(3)], axis=0)
    turned = jnp.concatenate(
        [jnp.concatenate([w_ref[3 * (2 - a) + 2 - b] for b in range(3)], axis=1) for a in range(3)], axis=0)
    turned = jnp.concatenate([turned, jnp.zeros((3 * CH, 256 - 3 * CH), F32)], axis=1)
    turned = jnp.concatenate([turned, jnp.zeros((256 - 3 * CH, 256), F32)], axis=0)
    adjoint = turned.T[:3 * CH, :3 * CH]
    fwd_hi, fwd_lo = split(forward)
    adj_hi, adj_lo = split(adjoint)

    def product(out, ref, hi, lo, left, right):
        rhs = jnp.concatenate([ref[left], ref[right]], axis=1)
        rhs_hi, rhs_lo = rhs[:3 * CH], rhs[3 * CH:]
        value = dot_nn(hi, rhs_hi) + dot_nn(lo, rhs_hi) + dot_nn(hi, rhs_lo)
        out[left] = value[:, :ROWS]
        out[right] = value[:, ROWS:]

    def products(out, ref, hi, lo):
        def step(s, carry):
            product(out, ref, hi, lo, 2 * s + 1, 2 * s + 2)
            return carry
        lax.fori_loop(0, COLS // 2, step, 0, unroll=4)


    remote(colout.at[0], colin.at[1], hs_sem.at[2], hr_sem.at[3], west).wait_recv()
    remote(colout.at[1], colin.at[0], hs_sem.at[3], hr_sem.at[2], east).wait_recv()

    build(z, 0, colin[0, :CH])
    build(z, COLS + 1, colin[1, :CH])
    blank = jnp.zeros((CH, ROWS), BF16)
    outer = []
    for low in range(2):
        r = (1 + 3 * low) * CH
        outer.append(jnp.concatenate([
            jnp.concatenate([v[1, r:r + CH], blank], axis=1),
            jnp.concatenate([blank, blank], axis=1),
            jnp.concatenate([blank, v[COLS, r:r + CH]], axis=1)], axis=0))
    for low in range(2):
        r = 3 * CH * low
        outer.append(jnp.concatenate([z[0, r:r + 3 * CH], z[COLS + 1, r:r + 3 * CH]], axis=1))
    acc = acc + weight_step(*outer)

    def packed(value, left):
        hi = value.astype(BF16).astype(F32)
        lo = (value - hi).astype(BF16).astype(F32)
        first, second = (lo, hi) if left else (hi, lo)
        return jnp.concatenate([hi + pltpu.roll(first, 64, 1), second], axis=1).astype(BF16)

    own = edge[...]
    inside = lane < 64
    left_rows = []
    for b in (-1, 0, 1):
        value = pltpu.roll(own, (64 + 2 * b) % 128, 1)
        if b == 1:
            value = jnp.where(lane < 2, pltpu.roll(colin[0, CH:], 1, 1), value)
        if b == -1:
            value = jnp.where(lane >= 62, pltpu.roll(colin[1, CH:], 63, 1), value)
        left_rows.append(packed(jnp.where(inside, value, 0.0), True))
    remote(edge, halo.at[0], hs_sem.at[0], hr_sem.at[0], north).wait_recv()
    remote(edge, halo.at[1], hs_sem.at[1], hr_sem.at[1], south).wait_recv()
    beyond = jnp.where(
        lane % 2 == 0,
        pltpu.roll(halo[1], 1 + is_south, 1),
        pltpu.roll(halo[0], 3 - is_north, 1),
    )
    corner[...] = beyond
    across = pltpu.roll(beyond, 126, 1)
    right_rows = [
        packed(jnp.where(inside & (lane % 2 == 1), across, 0.0), False),
        jnp.zeros((CH, 256), BF16),
        packed(jnp.where(inside & (lane % 2 == 0), across, 0.0), False),
    ]
    acc = acc + dot_nt(jnp.concatenate(left_rows, axis=0), jnp.concatenate(right_rows, axis=0))

    part[:3 * CH] = acc[:, :128]
    tail = jnp.concatenate([acc[:, 128:], jnp.zeros((3 * CH, 112), F32)], axis=1)
    part[3 * CH:] = (tail[:CH] + pltpu.roll(tail[CH:2 * CH], 16, 1)
                     + pltpu.roll(tail[2 * CH:], 32, 1))

    def chunk(seat):
        return pl.ds(pl.multiple_of(seat * PART, 8), PART)

    def scatter(to):
        return remote(part.at[chunk(to)], pooled.at[rank], as_sem.at[0, to], ar_sem.at[0, rank], pool(to))

    def exchange(slots, stage, way, to):
        own = slots.at[stage - 1, seats[way]]
        line = 2 * stage - 1 if slots is thick else 2 * stage
        return remote(own, own, as_sem.at[line, to], ar_sem.at[line, seats[way]], along(way, to))

    def exchanged(slots, stage, way, by):
        line = 2 * stage - 1 if slots is thick else 2 * stage
        spot = slots.at[stage - 1, by]
        return remote(spot, spot, as_sem.at[line, by], ar_sem.at[line, by], along(way, by))

    def gather(to):
        return remote(whole.at[chunk(rank)], whole.at[chunk(rank)], as_sem.at[5, to], ar_sem.at[5, rank], pool(to))

    def total(slots):
        value = slots[0]
        for k in range(1, 8):
            value = value + slots[k]
        return value

    def share(stage, thick_value, thin_value):
        ways = (0, 1) if stage == 1 else (1, 0)
        thick[stage - 1, seats[ways[0]]] = thick_value
        thin[stage - 1, seats[ways[1]]] = thin_value
        lines = [[(slots, way, to) for to in others(seats[way])] for slots, way in zip((thick, thin), ways)]
        for pair in zip(*lines):
            for slots, way, to in pair:
                exchange(slots, stage, way, to).start()

    def settle(stage):
        ways = (0, 1) if stage == 1 else (1, 0)
        for slots, way in zip((thick, thin), ways):
            for to in others(seats[way]):
                exchange(slots, stage, way, to).wait_send()

    def collect(stage):
        ways = (0, 1) if stage == 1 else (1, 0)
        for slots, way in zip((thick, thin), ways):
            for by in others(seats[way]):
                exchanged(slots, stage, way, by).wait_recv()
        return total(thick.at[stage - 1]), total(thin.at[stage - 1])

    corners_out = [
        remote(corner, cornerin.at[1], hs_sem.at[4], hr_sem.at[5], west),
        remote(corner, cornerin.at[0], hs_sem.at[5], hr_sem.at[4], east),
    ]
    for to in others(rank):
        scatter(to).start()
    pooled[rank] = part[chunk(rank)]
    for copy in corners_out:
        copy.start()

    products(p, z, fwd_hi, fwd_lo)
    product(p, z, fwd_hi, fwd_lo, 0, COLS + 1)

    for by in others(rank):
        remote(pooled.at[by], pooled.at[by], as_sem.at[0, by], ar_sem.at[0, by], pool(by)).wait_recv()
    sums = total(pooled)
    share(1, sums[:THICK], sums[THICK:])

    build(v, 0, colin[0, CH:])
    build(v, COLS + 1, colin[1, CH:])
    products(q, v, adj_hi, adj_lo)
    product(q, v, adj_hi, adj_lo, 0, COLS + 1)

    remote(corner, cornerin.at[1], hs_sem.at[4], hr_sem.at[5], west).wait_recv()
    remote(corner, cornerin.at[0], hs_sem.at[5], hr_sem.at[4], east).wait_recv()
    from_west, from_east = cornerin[0], cornerin[1]

    def finish(out, src, kernel_n, kernel_s, ring):
        weight_hi, weight_lo = split(jnp.concatenate([kernel_n, kernel_s], axis=1))
        odd = lane % 2 == 1
        ring_hi, ring_lo = split(jnp.concatenate(
            [jnp.where(odd, ring, 0.0), jnp.where(odd, 0.0, ring)], axis=0))
        terms = dot_nn(weight_hi, ring_hi) + dot_nn(weight_lo, ring_hi) + dot_nn(weight_hi, ring_lo)
        terms = (pltpu.roll(terms[:CH], 2, 1) + terms[CH:2 * CH]
                 + pltpu.roll(terms[2 * CH:], ROWS - 2, 1))
        rim = (lane == 0) | (lane == ROWS - 1)

        def step(j, carry):
            value = src[j, :CH] + src[j + 1, CH:2 * CH] + src[j + 2, 2 * CH:]
            value = value + jnp.where(rim, pltpu.roll(terms, 125 - 2 * j, 1), 0.0)
            out[pl.ds(j, CH, stride=COLS), :] = value
            return carry

        lax.fori_loop(0, COLS, step, 0, unroll=8)

    middle = (lane >= 2) & (lane < 66)
    ring_f = jnp.where(middle, beyond, jnp.where(
        lane < 2, pltpu.roll(from_west, 64, 1), pltpu.roll(from_east, 64, 1)))
    finish(resp, p, forward[:, :CH], forward[:, 2 * CH:], ring_f)

    for copy in halo_out + corners_out:
        copy.wait_send()
    for to in others(rank):
        scatter(to).wait_send()
    share(2, *collect(1))

    low_side, high_side = adjoint[:, :CH], adjoint[:, 2 * CH:]
    ring_g = jnp.where(middle, pltpu.roll(beyond, 64, 1), jnp.where(lane < 2, from_west, from_east))
    finish(gfield, q, jnp.where(lat == 0, high_side, low_side),
           jnp.where(lat == n_lat - 1, low_side, high_side), ring_g)

    settle(1)
    whole[chunk(rank)] = jnp.concatenate(collect(2), axis=0)
    for to in others(rank):
        gather(to).start()
    settle(2)
    for by in others(rank):
        remote(whole.at[chunk(by)], whole.at[chunk(by)], as_sem.at[5, by], ar_sem.at[5, by], pool(by)).wait_recv()
    final[...] = whole[...]
    for to in others(rank):
        gather(to).wait_send()


def hand_over(scale, resp, gfield, final, resp_hbm, gfield_hbm, gw_hbm, gw, sem):
    stores = [
        pltpu.make_async_copy(resp, resp_hbm, sem.at[0]),
        pltpu.make_async_copy(gfield, gfield_hbm, sem.at[1]),
        pltpu.make_async_copy(gw, gw_hbm, sem.at[2]),
    ]
    stores[0].start()
    stores[1].start()
    lane = lax.broadcasted_iota(jnp.int32, (CH, ROWS), 1)
    rest = final[3 * CH:]
    for b in range(3):
        rows = final[b * CH:(b + 1) * CH] * scale
        extra = pltpu.roll(rest, (32 - 16 * b) % 128, 1) * scale
        gw[b] = rows[:, :CH]
        gw[3 + b] = pltpu.roll(rows, 80, 1)[:, :CH]
        gw[6 + b] = jnp.where(lane < 32, pltpu.roll(rows, 32, 1), extra)[:, :CH]
    stores[2].start()
    for copy in stores:
        copy.wait()


def body(state_field, weight_bank, cotangent):
    cells = CH * COLS
    total_cells = ROWS * lax.axis_size("lat") * COLS * lax.axis_size("lon")
    near = pl.BlockSpec(memory_space=pltpu.VMEM)
    far = pl.BlockSpec(memory_space=pltpu.HBM)
    field = jax.ShapeDtypeStruct((cells, ROWS), F32)
    held = lambda *dims: pltpu.VMEM(dims, F32)
    pinned = lambda value: pltpu.with_memory_space_constraint(value, pltpu.HBM)
    parts = pl.pallas_call(
        kernel,
        out_shape=[held(cells, ROWS), held(cells, ROWS), held(8 * PART, ROWS)],
        in_specs=[far, far, far],
        out_specs=[near, near, near],
        scratch_shapes=[
            pltpu.VMEM((cells, ROWS), F32),
            pltpu.VMEM((cells, ROWS), F32),
            pltpu.VMEM((9, CH, CH), F32),
            pltpu.VMEM((COLS + 2, 6 * CH, ROWS), BF16),
            pltpu.VMEM((COLS + 2, 6 * CH, ROWS), BF16),
            pltpu.VMEM((COLS + 2, 3 * CH, ROWS), F32),
            pltpu.VMEM((COLS + 2, 3 * CH, ROWS), F32),
            pltpu.VMEM((CH, ROWS), F32),
            pltpu.VMEM((2, CH, ROWS), F32),
            pltpu.VMEM((2, 2 * CH, ROWS), F32),
            pltpu.VMEM((2, 2 * CH, ROWS), F32),
            pltpu.VMEM((CH, ROWS), F32),
            pltpu.VMEM((2, CH, ROWS), F32),
            pltpu.VMEM((8 * PART, ROWS), F32),
            pltpu.VMEM((8, PART, ROWS), F32),
            pltpu.VMEM((2, 8, THICK, ROWS), F32),
            pltpu.VMEM((2, 8, PART - THICK, ROWS), F32),
            pltpu.VMEM((8 * PART, ROWS), F32),
            pltpu.SemaphoreType.DMA((3,)),
            pltpu.SemaphoreType.DMA((6,)),
            pltpu.SemaphoreType.DMA((6,)),
            pltpu.SemaphoreType.DMA((6, 8)),
            pltpu.SemaphoreType.DMA((6, 8)),
        ],
        compiler_params=pltpu.CompilerParams(
            collective_id=0, has_side_effects=True, vmem_limit_bytes=40 << 20
        ),
        cost_estimate=pl.CostEstimate(
            flops=3 * 3 * 9 * CH * CH * COLS * ROWS * 2, bytes_accessed=16 * cells * ROWS, transcendentals=0
        ),
    )(pinned(state_field.reshape(cells, ROWS)), pinned(cotangent.reshape(cells, ROWS)), pinned(weight_bank))
    response, grad_field, grad_weight = pl.pallas_call(
        functools.partial(hand_over, 1.0 / math.sqrt(total_cells)),
        out_shape=[field, field, jax.ShapeDtypeStruct((9, CH, CH), F32)],
        in_specs=[near, near, near],
        out_specs=[far, far, far],
        scratch_shapes=[pltpu.VMEM((9, CH, CH), F32), pltpu.SemaphoreType.DMA((3,))],
    )(*[pltpu.with_memory_space_constraint(value, pltpu.VMEM) for value in parts])
    shape = (CH, COLS, ROWS)
    return response.reshape(shape), grad_field.reshape(shape), grad_weight


def solution(mesh):
    in_specs = (P(None, "lon", "lat"), P(), P(None, "lon", "lat"))
    out_specs = (P(None, "lon", "lat"), P(None, "lon", "lat"), P())
    return jax.shard_map(body, mesh=mesh, in_specs=in_specs, out_specs=out_specs, check_vma=False)
```

```python
import functools
import math

import jax
import jax.numpy as jnp
from jax import lax
from jax.experimental import pallas as pl
from jax.experimental.pallas import tpu as pltpu
from jax.sharding import PartitionSpec as P

CH = 48
COLS = 32
ROWS = 128
PART = 24
THICK = 16
MESH = pl.DeviceIdType.MESH
F32 = jnp.float32
BF16 = jnp.bfloat16


def split(x):
    hi = x.astype(BF16)
    return hi, (x - hi.astype(F32)).astype(BF16)


def column(ref, j):
    return ref[pl.ds(j, CH, stride=COLS), :]


def dot_nn(a, b):
    return lax.dot_general(a, b, (((1,), (0,)), ((), ())), preferred_element_type=F32)


def dot_nt(a, b):
    return lax.dot_general(a, b, (((1,), (1,)), ((), ())), preferred_element_type=F32)


def remote(src, dst, send, recv, to):
    return pltpu.make_async_remote_copy(
        src_ref=src, dst_ref=dst, send_sem=send, recv_sem=recv,
        device_id=to, device_id_type=MESH,
    )


def kernel(f_hbm, g_hbm, w_hbm, resp, gfield, final,
           fv, gv, w_ref, z, v, p, q, edge, halo, colout, colin, corner, cornerin,
           part, pooled, thick, thin, in_sem, hs_sem, hr_sem, as_sem, ar_sem):
    lon = lax.axis_index("lon")
    lat = lax.axis_index("lat")
    n_lon = lax.axis_size("lon")
    n_lat = lax.axis_size("lat")
    y, zh, core = lon // 8, (lon // 2) % 4, lon % 2
    x, zl = lat // 2, lat % 2
    depth = zh * 2 + zl
    is_north = jnp.where(lat == 0, 1, 0)
    is_south = jnp.where(lat == n_lat - 1, 1, 0)
    opposite = (lon + n_lon // 2) % n_lon

    def place(x, y, depth, core):
        return (y * 8 + (depth // 2) * 2 + core, x * 2 + depth % 2)

    west = ((lon + n_lon - 1) % n_lon, lat)
    east = ((lon + 1) % n_lon, lat)
    north = (jnp.where(lat == 0, opposite, lon), jnp.where(lat == 0, 0, lat - 1))
    south = (jnp.where(lat == n_lat - 1, opposite, lon),
             jnp.where(lat == n_lat - 1, n_lat - 1, lat + 1))
    rank = x * 2 + core

    def others(own):
        return [k + jnp.where(own <= k, 1, 0) for k in range(7)]

    first_is_y = core == 0
    seats = (jnp.where(first_is_y, y, depth), jnp.where(first_is_y, depth, y))

    def along(way, seat):
        by_y = first_is_y if way == 0 else jnp.logical_not(first_is_y)
        return place(x, jnp.where(by_y, seat, y), jnp.where(by_y, depth, seat), core)

    def pool(seat):
        return place(seat // 2, y, depth, seat % 2)

    barrier = pltpu.get_barrier_semaphore()
    partners = [west, east, north, south] + [pool(k) for k in others(rank)]
    partners += [along(way, k) for way in range(2) for k in others(seats[way])]
    load_f = pltpu.make_async_copy(f_hbm, fv, in_sem.at[0])
    load_g = pltpu.make_async_copy(g_hbm, gv, in_sem.at[1])
    load_w = pltpu.make_async_copy(w_hbm, w_ref, in_sem.at[2])
    load_f.start()
    load_g.start()
    load_w.start()
    for to in partners:
        pl.semaphore_signal(barrier, inc=1, device_id=to, device_id_type=MESH)
    v[0] = jnp.zeros((6 * CH, ROWS), BF16)
    v[COLS + 1] = jnp.zeros((6 * CH, ROWS), BF16)
    lane = lax.broadcasted_iota(jnp.int32, (CH, ROWS), 1)

    def pack(src, base, acc):
        def step(j, acc):
            return jnp.where(lane // 2 == j + base // 2, pltpu.roll(column(src, j), (2 * j + base + 1) % 128, 1), acc)
        return lax.fori_loop(0, COLS, step, acc, unroll=16)

    load_f.wait()
    packed_f = pack(fv, 0, jnp.zeros((CH, ROWS), F32))
    load_g.wait()
    edge[...] = pack(gv, 64, packed_f)
    for side, j in enumerate((0, COLS - 1)):
        colout[side, :CH] = column(fv, j)
        colout[side, CH:] = column(gv, j)

    def put(ref, at, a, value):
        hi, lo = split(value)
        ref[at, a * CH:(a + 1) * CH] = hi
        ref[at, (3 + a) * CH:(4 + a) * CH] = lo

    def build(ref, at, value):
        put(ref, at, 0, jnp.where(lane == 0, 0.0, pltpu.roll(value, 1, 1)))
        put(ref, at, 1, value)
        put(ref, at, 2, jnp.where(lane == ROWS - 1, 0.0, pltpu.roll(value, ROWS - 1, 1)))

    def build_all(ref, src):
        def step(j, carry):
            build(ref, j + 1, column(src, j))
            return carry
        lax.fori_loop(0, COLS, step, 0, unroll=8)

    pl.semaphore_wait(barrier, len(partners))

    from_north = jnp.where(lat == 0, 0, 1)
    from_south = jnp.where(lat == n_lat - 1, 1, 0)
    halo_out = [
        remote(colout.at[0], colin.at[1], hs_sem.at[2], hr_sem.at[3], west),
        remote(colout.at[1], colin.at[0], hs_sem.at[3], hr_sem.at[2], east),
        remote(edge, halo.at[from_north], hs_sem.at[0], hr_sem.at[from_north], north),
        remote(edge, halo.at[from_south], hs_sem.at[1], hr_sem.at[from_south], south),
    ]
    for copy in halo_out:
        copy.start()

    build_all(z, fv)
    build_all(v, gv)

    def weight_step(lhs_hi, lhs_lo, rhs_hi, rhs_lo):
        return dot_nt(lhs_hi, rhs_hi) + dot_nt(lhs_lo, rhs_hi) + dot_nt(lhs_hi, rhs_lo)

    def local_weight(s, acc):
        sides = [[], [], [], []]
        for k in range(16):
            at = s * 16 + k + 1
            for low in range(2):
                r = (1 + 3 * low) * CH
                sides[low].append(jnp.concatenate(
                    [v[at + 1, r:r + CH], v[at, r:r + CH], v[at - 1, r:r + CH]], axis=0))
                sides[2 + low].append(z[at, 3 * CH * low:3 * CH * (low + 1)])
        return acc + weight_step(*[jnp.concatenate(s, axis=1) for s in sides])

    acc = lax.fori_loop(0, COLS // 16, local_weight, jnp.zeros((3 * CH, 3 * CH), F32))

    load_w.wait()
    forward = jnp.concatenate(
        [jnp.concatenate([w_ref[3 * a + b] for a in range(3)], axis=1) for b in range(3)], axis=0)
    turned = jnp.concatenate(
        [jnp.concatenate([w_ref[3 * (2 - a) + 2 - b] for b in range(3)], axis=1) for a in range(3)], axis=0)
    turned = jnp.concatenate([turned, jnp.zeros((3 * CH, 256 - 3 * CH), F32)], axis=1)
    turned = jnp.concatenate([turned, jnp.zeros((256 - 3 * CH, 256), F32)], axis=0)
    adjoint = turned.T[:3 * CH, :3 * CH]
    fwd_hi, fwd_lo = split(forward)
    adj_hi, adj_lo = split(adjoint)

    def product(out, ref, hi, lo, left, right):
        rhs = jnp.concatenate([ref[left], ref[right]], axis=1)
        rhs_hi, rhs_lo = rhs[:3 * CH], rhs[3 * CH:]
        value = dot_nn(hi, rhs_hi) + dot_nn(lo, rhs_hi) + dot_nn(hi, rhs_lo)
        out[left] = value[:, :ROWS]
        out[right] = value[:, ROWS:]

    def products(out, ref, hi, lo):
        def step(s, carry):
            product(out, ref, hi, lo, 2 * s + 1, 2 * s + 2)
            return carry
        lax.fori_loop(0, COLS // 2, step, 0, unroll=4)


    remote(colout.at[0], colin.at[1], hs_sem.at[2], hr_sem.at[3], west).wait_recv()
    remote(colout.at[1], colin.at[0], hs_sem.at[3], hr_sem.at[2], east).wait_recv()

    build(z, 0, colin[0, :CH])
    build(z, COLS + 1, colin[1, :CH])
    blank = jnp.zeros((CH, ROWS), BF16)
    outer = []
    for low in range(2):
        r = (1 + 3 * low) * CH
        outer.append(jnp.concatenate([
            jnp.concatenate([v[1, r:r + CH], blank], axis=1),
            jnp.concatenate([blank, blank], axis=1),
            jnp.concatenate([blank, v[COLS, r:r + CH]], axis=1)], axis=0))
    for low in range(2):
        r = 3 * CH * low
        outer.append(jnp.concatenate([z[0, r:r + 3 * CH], z[COLS + 1, r:r + 3 * CH]], axis=1))
    acc = acc + weight_step(*outer)

    def packed(value, left):
        hi = value.astype(BF16).astype(F32)
        lo = (value - hi).astype(BF16).astype(F32)
        first, second = (lo, hi) if left else (hi, lo)
        return jnp.concatenate([hi + pltpu.roll(first, 64, 1), second], axis=1).astype(BF16)

    own = edge[...]
    inside = lane < 64
    left_rows = []
    for b in (-1, 0, 1):
        value = pltpu.roll(own, (64 + 2 * b) % 128, 1)
        if b == 1:
            value = jnp.where(lane < 2, pltpu.roll(colin[0, CH:], 1, 1), value)
        if b == -1:
            value = jnp.where(lane >= 62, pltpu.roll(colin[1, CH:], 63, 1), value)
        left_rows.append(packed(jnp.where(inside, value, 0.0), True))
    remote(edge, halo.at[0], hs_sem.at[0], hr_sem.at[0], north).wait_recv()
    remote(edge, halo.at[1], hs_sem.at[1], hr_sem.at[1], south).wait_recv()
    beyond = jnp.where(
        lane % 2 == 0,
        pltpu.roll(halo[1], 1 + is_south, 1),
        pltpu.roll(halo[0], 3 - is_north, 1),
    )
    corner[...] = beyond
    across = pltpu.roll(beyond, 126, 1)
    right_rows = [
        packed(jnp.where(inside & (lane % 2 == 1), across, 0.0), False),
        jnp.zeros((CH, 256), BF16),
        packed(jnp.where(inside & (lane % 2 == 0), across, 0.0), False),
    ]
    acc = acc + dot_nt(jnp.concatenate(left_rows, axis=0), jnp.concatenate(right_rows, axis=0))

    part[:3 * CH] = acc[:, :128]

    def chunk(seat):
        return pl.ds(pl.multiple_of(seat * PART, 8), PART)

    def scatter(to):
        return remote(part.at[chunk(to)], pooled.at[rank], as_sem.at[0, to], ar_sem.at[0, rank], pool(to))

    def exchange(slots, stage, way, to):
        own = slots.at[stage - 1, seats[way]]
        line = 2 * stage - 1 if slots is thick else 2 * stage
        return remote(own, own, as_sem.at[line, to], ar_sem.at[line, seats[way]], along(way, to))

    def exchanged(slots, stage, way, by):
        line = 2 * stage - 1 if slots is thick else 2 * stage
        spot = slots.at[stage - 1, by]
        return remote(spot, spot, as_sem.at[line, by], ar_sem.at[line, by], along(way, by))

    def gather(to):
        return remote(final.at[chunk(rank)], final.at[chunk(rank)], as_sem.at[5, to], ar_sem.at[5, rank], pool(to))

    def total(slots):
        value = slots[0]
        for k in range(1, 8):
            value = value + slots[k]
        return value

    def share(stage, thick_value, thin_value):
        ways = (0, 1) if stage == 1 else (1, 0)
        thick[stage - 1, seats[ways[0]]] = thick_value
        thin[stage - 1, seats[ways[1]]] = thin_value
        lines = [[(slots, way, to) for to in others(seats[way])] for slots, way in zip((thick, thin), ways)]
        for pair in zip(*lines):
            for slots, way, to in pair:
                exchange(slots, stage, way, to).start()

    def settle(stage):
        ways = (0, 1) if stage == 1 else (1, 0)
        for slots, way in zip((thick, thin), ways):
            for to in others(seats[way]):
                exchange(slots, stage, way, to).wait_send()

    def collect(stage):
        ways = (0, 1) if stage == 1 else (1, 0)
        for slots, way in zip((thick, thin), ways):
            for by in others(seats[way]):
                exchanged(slots, stage, way, by).wait_recv()
        return total(thick.at[stage - 1]), total(thin.at[stage - 1])

    corners_out = [
        remote(corner, cornerin.at[1], hs_sem.at[4], hr_sem.at[5], west),
        remote(corner, cornerin.at[0], hs_sem.at[5], hr_sem.at[4], east),
    ]
    for to in others(rank)[:5]:
        scatter(to).start()
    tail = jnp.concatenate([acc[:, 128:], jnp.zeros((3 * CH, 112), F32)], axis=1)
    part[3 * CH:] = (tail[:CH] + pltpu.roll(tail[CH:2 * CH], 16, 1)
                     + pltpu.roll(tail[2 * CH:], 32, 1))
    for to in others(rank)[5:]:
        scatter(to).start()
    pooled[rank] = part[chunk(rank)]
    for copy in corners_out:
        copy.start()

    products(p, z, fwd_hi, fwd_lo)
    product(p, z, fwd_hi, fwd_lo, 0, COLS + 1)

    for by in others(rank):
        remote(pooled.at[by], pooled.at[by], as_sem.at[0, by], ar_sem.at[0, by], pool(by)).wait_recv()
    sums = total(pooled)
    share(1, sums[:THICK], sums[THICK:])

    build(v, 0, colin[0, CH:])
    build(v, COLS + 1, colin[1, CH:])
    products(q, v, adj_hi, adj_lo)
    product(q, v, adj_hi, adj_lo, 0, COLS + 1)

    remote(corner, cornerin.at[1], hs_sem.at[4], hr_sem.at[5], west).wait_recv()
    remote(corner, cornerin.at[0], hs_sem.at[5], hr_sem.at[4], east).wait_recv()
    from_west, from_east = cornerin[0], cornerin[1]

    def finish(out, src, kernel_n, kernel_s, ring):
        weight_hi, weight_lo = split(jnp.concatenate([kernel_n, kernel_s], axis=1))
        odd = lane % 2 == 1
        ring_hi, ring_lo = split(jnp.concatenate(
            [jnp.where(odd, ring, 0.0), jnp.where(odd, 0.0, ring)], axis=0))
        terms = dot_nn(weight_hi, ring_hi) + dot_nn(weight_lo, ring_hi) + dot_nn(weight_hi, ring_lo)
        terms = (pltpu.roll(terms[:CH], 2, 1) + terms[CH:2 * CH]
                 + pltpu.roll(terms[2 * CH:], ROWS - 2, 1))
        rim = (lane == 0) | (lane == ROWS - 1)

        def step(j, carry):
            value = src[j, :CH] + src[j + 1, CH:2 * CH] + src[j + 2, 2 * CH:]
            value = value + jnp.where(rim, pltpu.roll(terms, 125 - 2 * j, 1), 0.0)
            out[pl.ds(j, CH, stride=COLS), :] = value
            return carry

        lax.fori_loop(0, COLS, step, 0, unroll=8)

    middle = (lane >= 2) & (lane < 66)
    ring_f = jnp.where(middle, beyond, jnp.where(
        lane < 2, pltpu.roll(from_west, 64, 1), pltpu.roll(from_east, 64, 1)))
    finish(resp, p, forward[:, :CH], forward[:, 2 * CH:], ring_f)

    for copy in halo_out + corners_out:
        copy.wait_send()
    for to in others(rank):
        scatter(to).wait_send()
    share(2, *collect(1))

    low_side, high_side = adjoint[:, :CH], adjoint[:, 2 * CH:]
    ring_g = jnp.where(middle, pltpu.roll(beyond, 64, 1), jnp.where(lane < 2, from_west, from_east))
    finish(gfield, q, jnp.where(lat == 0, high_side, low_side),
           jnp.where(lat == n_lat - 1, low_side, high_side), ring_g)

    settle(1)
    final[chunk(rank)] = jnp.concatenate(collect(2), axis=0)
    for to in others(rank):
        gather(to).start()
    settle(2)
    for by in others(rank):
        remote(final.at[chunk(by)], final.at[chunk(by)], as_sem.at[5, by], ar_sem.at[5, by], pool(by)).wait_recv()
    for to in others(rank):
        gather(to).wait_send()


def hand_over(scale, resp, gfield, final, resp_hbm, gfield_hbm, gw_hbm, gw, sem):
    stores = [
        pltpu.make_async_copy(resp, resp_hbm, sem.at[0]),
        pltpu.make_async_copy(gfield, gfield_hbm, sem.at[1]),
        pltpu.make_async_copy(gw, gw_hbm, sem.at[2]),
    ]
    stores[0].start()
    stores[1].start()
    lane = lax.broadcasted_iota(jnp.int32, (CH, ROWS), 1)
    rest = final[3 * CH:]
    for b in range(3):
        rows = final[b * CH:(b + 1) * CH] * scale
        extra = pltpu.roll(rest, (32 - 16 * b) % 128, 1) * scale
        gw[b] = rows[:, :CH]
        gw[3 + b] = pltpu.roll(rows, 80, 1)[:, :CH]
        gw[6 + b] = jnp.where(lane < 32, pltpu.roll(rows, 32, 1), extra)[:, :CH]
    stores[2].start()
    for copy in stores:
        copy.wait()


def body(state_field, weight_bank, cotangent):
    cells = CH * COLS
    total_cells = ROWS * lax.axis_size("lat") * COLS * lax.axis_size("lon")
    near = pl.BlockSpec(memory_space=pltpu.VMEM)
    far = pl.BlockSpec(memory_space=pltpu.HBM)
    field = jax.ShapeDtypeStruct((cells, ROWS), F32)
    held = lambda *dims: pltpu.VMEM(dims, F32)
    pinned = lambda value: pltpu.with_memory_space_constraint(value, pltpu.HBM)
    parts = pl.pallas_call(
        kernel,
        out_shape=[held(cells, ROWS), held(cells, ROWS), held(8 * PART, ROWS)],
        in_specs=[far, far, far],
        out_specs=[near, near, near],
        scratch_shapes=[
            pltpu.VMEM((cells, ROWS), F32),
            pltpu.VMEM((cells, ROWS), F32),
            pltpu.VMEM((9, CH, CH), F32),
            pltpu.VMEM((COLS + 2, 6 * CH, ROWS), BF16),
            pltpu.VMEM((COLS + 2, 6 * CH, ROWS), BF16),
            pltpu.VMEM((COLS + 2, 3 * CH, ROWS), F32),
            pltpu.VMEM((COLS + 2, 3 * CH, ROWS), F32),
            pltpu.VMEM((CH, ROWS), F32),
            pltpu.VMEM((2, CH, ROWS), F32),
            pltpu.VMEM((2, 2 * CH, ROWS), F32),
            pltpu.VMEM((2, 2 * CH, ROWS), F32),
            pltpu.VMEM((CH, ROWS), F32),
            pltpu.VMEM((2, CH, ROWS), F32),
            pltpu.VMEM((8 * PART, ROWS), F32),
            pltpu.VMEM((8, PART, ROWS), F32),
            pltpu.VMEM((2, 8, THICK, ROWS), F32),
            pltpu.VMEM((2, 8, PART - THICK, ROWS), F32),
            pltpu.SemaphoreType.DMA((3,)),
            pltpu.SemaphoreType.DMA((6,)),
            pltpu.SemaphoreType.DMA((6,)),
            pltpu.SemaphoreType.DMA((6, 8)),
            pltpu.SemaphoreType.DMA((6, 8)),
        ],
        compiler_params=pltpu.CompilerParams(
            collective_id=0, has_side_effects=True, vmem_limit_bytes=40 << 20
        ),
        cost_estimate=pl.CostEstimate(
            flops=3 * 3 * 9 * CH * CH * COLS * ROWS * 2, bytes_accessed=16 * cells * ROWS, transcendentals=0
        ),
    )(pinned(state_field.reshape(cells, ROWS)), pinned(cotangent.reshape(cells, ROWS)), pinned(weight_bank))
    response, grad_field, grad_weight = pl.pallas_call(
        functools.partial(hand_over, 1.0 / math.sqrt(total_cells)),
        out_shape=[field, field, jax.ShapeDtypeStruct((9, CH, CH), F32)],
        in_specs=[near, near, near],
        out_specs=[far, far, far],
        scratch_shapes=[pltpu.VMEM((9, CH, CH), F32), pltpu.SemaphoreType.DMA((3,))],
    )(*[pltpu.with_memory_space_constraint(value, pltpu.VMEM) for value in parts])
    shape = (CH, COLS, ROWS)
    return response.reshape(shape), grad_field.reshape(shape), grad_weight


def solution(mesh):
    in_specs = (P(None, "lon", "lat"), P(), P(None, "lon", "lat"))
    out_specs = (P(None, "lon", "lat"), P(None, "lon", "lat"), P())
    return jax.shard_map(body, mesh=mesh, in_specs=in_specs, out_specs=out_specs, check_vma=False)
```

```python
import functools
import math

import jax
import jax.numpy as jnp
from jax import lax
from jax.experimental import pallas as pl
from jax.experimental.pallas import tpu as pltpu
from jax.sharding import PartitionSpec as P

CH = 48
COLS = 32
ROWS = 128
PART = 24
THICK = 16
MESH = pl.DeviceIdType.MESH
F32 = jnp.float32
BF16 = jnp.bfloat16


def split(x):
    hi = x.astype(BF16)
    return hi, (x - hi.astype(F32)).astype(BF16)


def column(ref, j):
    return ref[pl.ds(j, CH, stride=COLS), :]


def dot_nn(a, b):
    return lax.dot_general(a, b, (((1,), (0,)), ((), ())), preferred_element_type=F32)


def dot_nt(a, b):
    return lax.dot_general(a, b, (((1,), (1,)), ((), ())), preferred_element_type=F32)


def remote(src, dst, send, recv, to):
    return pltpu.make_async_remote_copy(
        src_ref=src, dst_ref=dst, send_sem=send, recv_sem=recv,
        device_id=to, device_id_type=MESH,
    )


def kernel(f_hbm, g_hbm, w_hbm, resp, gfield, final,
           fv, gv, w_ref, z, v, p, q, edge, halo, colout, colin, corner, cornerin,
           part, pooled, thick, thin, in_sem, hs_sem, hr_sem, as_sem, ar_sem):
    lon = lax.axis_index("lon")
    lat = lax.axis_index("lat")
    n_lon = lax.axis_size("lon")
    n_lat = lax.axis_size("lat")
    y, zh, core = lon // 8, (lon // 2) % 4, lon % 2
    x, zl = lat // 2, lat % 2
    depth = zh * 2 + zl
    is_north = jnp.where(lat == 0, 1, 0)
    is_south = jnp.where(lat == n_lat - 1, 1, 0)
    opposite = (lon + n_lon // 2) % n_lon

    def place(x, y, depth, core):
        return (y * 8 + (depth // 2) * 2 + core, x * 2 + depth % 2)

    west = ((lon + n_lon - 1) % n_lon, lat)
    east = ((lon + 1) % n_lon, lat)
    north = (jnp.where(lat == 0, opposite, lon), jnp.where(lat == 0, 0, lat - 1))
    south = (jnp.where(lat == n_lat - 1, opposite, lon),
             jnp.where(lat == n_lat - 1, n_lat - 1, lat + 1))
    rank = x * 2 + core

    def others(own):
        return [k + jnp.where(own <= k, 1, 0) for k in range(7)]

    first_is_y = core == 0
    seats = (jnp.where(first_is_y, y, depth), jnp.where(first_is_y, depth, y))

    def along(way, seat):
        by_y = first_is_y if way == 0 else jnp.logical_not(first_is_y)
        return place(x, jnp.where(by_y, seat, y), jnp.where(by_y, depth, seat), core)

    def pool(seat):
        return place(seat // 2, y, depth, seat % 2)

    barrier = pltpu.get_barrier_semaphore()
    partners = [west, east, north, south] + [pool(k) for k in others(rank)]
    partners += [along(way, k) for way in range(2) for k in others(seats[way])]
    load_f = pltpu.make_async_copy(f_hbm, fv, in_sem.at[0])
    load_g = pltpu.make_async_copy(g_hbm, gv, in_sem.at[1])
    load_w = pltpu.make_async_copy(w_hbm, w_ref, in_sem.at[2])
    load_f.start()
    load_g.start()
    load_w.start()
    for to in partners:
        pl.semaphore_signal(barrier, inc=1, device_id=to, device_id_type=MESH)
    v[0] = jnp.zeros((6 * CH, ROWS), BF16)
    v[COLS + 1] = jnp.zeros((6 * CH, ROWS), BF16)
    lane = lax.broadcasted_iota(jnp.int32, (CH, ROWS), 1)

    def pack(src, base, acc):
        def step(j, acc):
            return jnp.where(lane // 2 == j + base // 2, pltpu.roll(column(src, j), (2 * j + base + 1) % 128, 1), acc)
        return lax.fori_loop(0, COLS, step, acc, unroll=COLS)

    load_f.wait()
    packed_f = pack(fv, 0, jnp.zeros((CH, ROWS), F32))
    load_g.wait()
    edge[...] = pack(gv, 64, packed_f)
    for side, j in enumerate((0, COLS - 1)):
        colout[side, :CH] = column(fv, j)
        colout[side, CH:] = column(gv, j)

    def put(ref, at, a, value):
        hi, lo = split(value)
        ref[at, a * CH:(a + 1) * CH] = hi
        ref[at, (3 + a) * CH:(4 + a) * CH] = lo

    def build(ref, at, value):
        put(ref, at, 0, jnp.where(lane == 0, 0.0, pltpu.roll(value, 1, 1)))
        put(ref, at, 1, value)
        put(ref, at, 2, jnp.where(lane == ROWS - 1, 0.0, pltpu.roll(value, ROWS - 1, 1)))

    def build_all(ref, src):
        def step(j, carry):
            build(ref, j + 1, column(src, j))
            return carry
        lax.fori_loop(0, COLS, step, 0, unroll=8)

    pl.semaphore_wait(barrier, len(partners))

    from_north = jnp.where(lat == 0, 0, 1)
    from_south = jnp.where(lat == n_lat - 1, 1, 0)
    halo_out = [
        remote(colout.at[0], colin.at[1], hs_sem.at[2], hr_sem.at[3], west),
        remote(colout.at[1], colin.at[0], hs_sem.at[3], hr_sem.at[2], east),
        remote(edge, halo.at[from_north], hs_sem.at[0], hr_sem.at[from_north], north),
        remote(edge, halo.at[from_south], hs_sem.at[1], hr_sem.at[from_south], south),
    ]
    for copy in halo_out:
        copy.start()

    build_all(z, fv)
    build_all(v, gv)

    def weight_step(lhs_hi, lhs_lo, rhs_hi, rhs_lo):
        return dot_nt(lhs_hi, rhs_hi) + dot_nt(lhs_lo, rhs_hi) + dot_nt(lhs_hi, rhs_lo)

    def local_weight(s, acc):
        sides = [[], [], [], []]
        for k in range(16):
            at = s * 16 + k + 1
            for low in range(2):
                r = (1 + 3 * low) * CH
                sides[low].append(jnp.concatenate(
                    [v[at + 1, r:r + CH], v[at, r:r + CH], v[at - 1, r:r + CH]], axis=0))
                sides[2 + low].append(z[at, 3 * CH * low:3 * CH * (low + 1)])
        return acc + weight_step(*[jnp.concatenate(s, axis=1) for s in sides])

    acc = lax.fori_loop(0, COLS // 16, local_weight, jnp.zeros((3 * CH, 3 * CH), F32))

    load_w.wait()
    forward = jnp.concatenate(
        [jnp.concatenate([w_ref[3 * a + b] for a in range(3)], axis=1) for b in range(3)], axis=0)
    turned = jnp.concatenate(
        [jnp.concatenate([w_ref[3 * (2 - a) + 2 - b] for b in range(3)], axis=1) for a in range(3)], axis=0)
    turned = jnp.concatenate([turned, jnp.zeros((3 * CH, 256 - 3 * CH), F32)], axis=1)
    turned = jnp.concatenate([turned, jnp.zeros((256 - 3 * CH, 256), F32)], axis=0)
    adjoint = turned.T[:3 * CH, :3 * CH]
    fwd_hi, fwd_lo = split(forward)
    adj_hi, adj_lo = split(adjoint)

    def product(out, ref, hi, lo, left, right):
        rhs = jnp.concatenate([ref[left], ref[right]], axis=1)
        rhs_hi, rhs_lo = rhs[:3 * CH], rhs[3 * CH:]
        value = dot_nn(hi, rhs_hi) + dot_nn(lo, rhs_hi) + dot_nn(hi, rhs_lo)
        out[left] = value[:, :ROWS]
        out[right] = value[:, ROWS:]

    def products(out, ref, hi, lo):
        def step(s, carry):
            product(out, ref, hi, lo, 2 * s + 1, 2 * s + 2)
            return carry
        lax.fori_loop(0, COLS // 2, step, 0, unroll=4)


    remote(colout.at[0], colin.at[1], hs_sem.at[2], hr_sem.at[3], west).wait_recv()
    remote(colout.at[1], colin.at[0], hs_sem.at[3], hr_sem.at[2], east).wait_recv()

    build(z, 0, colin[0, :CH])
    build(z, COLS + 1, colin[1, :CH])
    blank = jnp.zeros((CH, ROWS), BF16)
    outer = []
    for low in range(2):
        r = (1 + 3 * low) * CH
        outer.append(jnp.concatenate([
            jnp.concatenate([v[1, r:r + CH], blank], axis=1),
            jnp.concatenate([blank, blank], axis=1),
            jnp.concatenate([blank, v[COLS, r:r + CH]], axis=1)], axis=0))
    for low in range(2):
        r = 3 * CH * low
        outer.append(jnp.concatenate([z[0, r:r + 3 * CH], z[COLS + 1, r:r + 3 * CH]], axis=1))
    acc = acc + weight_step(*outer)

    def packed(value, left):
        hi = value.astype(BF16).astype(F32)
        lo = (value - hi).astype(BF16).astype(F32)
        first, second = (lo, hi) if left else (hi, lo)
        return jnp.concatenate([hi + pltpu.roll(first, 64, 1), second], axis=1).astype(BF16)

    own = edge[...]
    inside = lane < 64
    left_rows = []
    for b in (-1, 0, 1):
        value = pltpu.roll(own, (64 + 2 * b) % 128, 1)
        if b == 1:
            value = jnp.where(lane < 2, pltpu.roll(colin[0, CH:], 1, 1), value)
        if b == -1:
            value = jnp.where(lane >= 62, pltpu.roll(colin[1, CH:], 63, 1), value)
        left_rows.append(packed(jnp.where(inside, value, 0.0), True))
    remote(edge, halo.at[0], hs_sem.at[0], hr_sem.at[0], north).wait_recv()
    remote(edge, halo.at[1], hs_sem.at[1], hr_sem.at[1], south).wait_recv()
    across = jnp.where(
        lane % 2 == 0,
        pltpu.roll(halo[1], (127 + is_south) % 128, 1),
        pltpu.roll(halo[0], 1 - is_north, 1),
    )
    right_rows = [
        packed(jnp.where(inside & (lane % 2 == 1), across, 0.0), False),
        jnp.zeros((CH, 256), BF16),
        packed(jnp.where(inside & (lane % 2 == 0), across, 0.0), False),
    ]
    acc = acc + dot_nt(jnp.concatenate(left_rows, axis=0), jnp.concatenate(right_rows, axis=0))

    part[:3 * CH] = acc[:, :128]

    def chunk(seat):
        return pl.ds(pl.multiple_of(seat * PART, 8), PART)

    def scatter(to):
        return remote(part.at[chunk(to)], pooled.at[rank], as_sem.at[0, to], ar_sem.at[0, rank], pool(to))

    def exchange(slots, stage, way, to):
        own = slots.at[stage - 1, seats[way]]
        line = 2 * stage - 1 if slots is thick else 2 * stage
        return remote(own, own, as_sem.at[line, to], ar_sem.at[line, seats[way]], along(way, to))

    def exchanged(slots, stage, way, by):
        line = 2 * stage - 1 if slots is thick else 2 * stage
        spot = slots.at[stage - 1, by]
        return remote(spot, spot, as_sem.at[line, by], ar_sem.at[line, by], along(way, by))

    def gather(to):
        return remote(final.at[chunk(rank)], final.at[chunk(rank)], as_sem.at[5, to], ar_sem.at[5, rank], pool(to))

    def total(slots):
        value = slots[0]
        for k in range(1, 8):
            value = value + slots[k]
        return value

    def share(stage, thick_value, thin_value):
        ways = (0, 1) if stage == 1 else (1, 0)
        thick[stage - 1, seats[ways[0]]] = thick_value
        thin[stage - 1, seats[ways[1]]] = thin_value
        lines = [[(slots, way, to) for to in others(seats[way])] for slots, way in zip((thick, thin), ways)]
        for pair in zip(*lines):
            for slots, way, to in pair:
                exchange(slots, stage, way, to).start()

    def settle(stage):
        ways = (0, 1) if stage == 1 else (1, 0)
        for slots, way in zip((thick, thin), ways):
            for to in others(seats[way]):
                exchange(slots, stage, way, to).wait_send()

    def collect(stage):
        ways = (0, 1) if stage == 1 else (1, 0)
        for slots, way in zip((thick, thin), ways):
            for by in others(seats[way]):
                exchanged(slots, stage, way, by).wait_recv()
        return total(thick.at[stage - 1]), total(thin.at[stage - 1])

    corners_out = [
        remote(corner, cornerin.at[1], hs_sem.at[4], hr_sem.at[5], west),
        remote(corner, cornerin.at[0], hs_sem.at[5], hr_sem.at[4], east),
    ]
    for to in others(rank)[:5]:
        scatter(to).start()
    tail = jnp.concatenate([acc[:, 128:], jnp.zeros((3 * CH, 112), F32)], axis=1)
    part[3 * CH:] = (tail[:CH] + pltpu.roll(tail[CH:2 * CH], 16, 1)
                     + pltpu.roll(tail[2 * CH:], 32, 1))
    for to in others(rank)[5:]:
        scatter(to).start()
    pooled[rank] = part[chunk(rank)]
    beyond = pltpu.roll(across, 2, 1)
    corner[...] = beyond
    for copy in corners_out:
        copy.start()

    products(p, z, fwd_hi, fwd_lo)
    product(p, z, fwd_hi, fwd_lo, 0, COLS + 1)

    for by in others(rank):
        remote(pooled.at[by], pooled.at[by], as_sem.at[0, by], ar_sem.at[0, by], pool(by)).wait_recv()
    sums = total(pooled)
    share(1, sums[:THICK], sums[THICK:])

    build(v, 0, colin[0, CH:])
    build(v, COLS + 1, colin[1, CH:])
    products(q, v, adj_hi, adj_lo)
    product(q, v, adj_hi, adj_lo, 0, COLS + 1)

    remote(corner, cornerin.at[1], hs_sem.at[4], hr_sem.at[5], west).wait_recv()
    remote(corner, cornerin.at[0], hs_sem.at[5], hr_sem.at[4], east).wait_recv()
    from_west, from_east = cornerin[0], cornerin[1]

    def finish(out, src, kernel_n, kernel_s, ring):
        weight_hi, weight_lo = split(jnp.concatenate([kernel_n, kernel_s], axis=1))
        odd = lane % 2 == 1
        ring_hi, ring_lo = split(jnp.concatenate(
            [jnp.where(odd, ring, 0.0), jnp.where(odd, 0.0, ring)], axis=0))
        terms = dot_nn(weight_hi, ring_hi) + dot_nn(weight_lo, ring_hi) + dot_nn(weight_hi, ring_lo)
        terms = (pltpu.roll(terms[:CH], 2, 1) + terms[CH:2 * CH]
                 + pltpu.roll(terms[2 * CH:], ROWS - 2, 1))
        rim = (lane == 0) | (lane == ROWS - 1)

        def step(j, carry):
            value = src[j, :CH] + src[j + 1, CH:2 * CH] + src[j + 2, 2 * CH:]
            value = value + jnp.where(rim, pltpu.roll(terms, 125 - 2 * j, 1), 0.0)
            out[pl.ds(j, CH, stride=COLS), :] = value
            return carry

        lax.fori_loop(0, COLS, step, 0, unroll=8)

    middle = (lane >= 2) & (lane < 66)
    ring_f = jnp.where(middle, beyond, jnp.where(
        lane < 2, pltpu.roll(from_west, 64, 1), pltpu.roll(from_east, 64, 1)))
    finish(resp, p, forward[:, :CH], forward[:, 2 * CH:], ring_f)

    for copy in halo_out + corners_out:
        copy.wait_send()
    for to in others(rank):
        scatter(to).wait_send()
    share(2, *collect(1))

    low_side, high_side = adjoint[:, :CH], adjoint[:, 2 * CH:]
    ring_g = jnp.where(middle, pltpu.roll(beyond, 64, 1), jnp.where(lane < 2, from_west, from_east))
    finish(gfield, q, jnp.where(lat == 0, high_side, low_side),
           jnp.where(lat == n_lat - 1, low_side, high_side), ring_g)

    settle(1)
    final[chunk(rank)] = jnp.concatenate(collect(2), axis=0)
    for to in others(rank):
        gather(to).start()
    settle(2)
    for by in others(rank):
        remote(final.at[chunk(by)], final.at[chunk(by)], as_sem.at[5, by], ar_sem.at[5, by], pool(by)).wait_recv()
    for to in others(rank):
        gather(to).wait_send()


def hand_over(scale, resp, gfield, final, resp_hbm, gfield_hbm, gw_hbm, gw, sem):
    stores = [
        pltpu.make_async_copy(resp, resp_hbm, sem.at[0]),
        pltpu.make_async_copy(gfield, gfield_hbm, sem.at[1]),
        pltpu.make_async_copy(gw, gw_hbm, sem.at[2]),
    ]
    stores[0].start()
    stores[1].start()
    lane = lax.broadcasted_iota(jnp.int32, (CH, ROWS), 1)
    rest = final[3 * CH:]
    for b in range(3):
        rows = final[b * CH:(b + 1) * CH] * scale
        extra = pltpu.roll(rest, (32 - 16 * b) % 128, 1) * scale
        gw[b] = rows[:, :CH]
        gw[3 + b] = pltpu.roll(rows, 80, 1)[:, :CH]
        gw[6 + b] = jnp.where(lane < 32, pltpu.roll(rows, 32, 1), extra)[:, :CH]
    stores[2].start()
    for copy in stores:
        copy.wait()


def body(state_field, weight_bank, cotangent):
    cells = CH * COLS
    total_cells = ROWS * lax.axis_size("lat") * COLS * lax.axis_size("lon")
    near = pl.BlockSpec(memory_space=pltpu.VMEM)
    far = pl.BlockSpec(memory_space=pltpu.HBM)
    field = jax.ShapeDtypeStruct((cells, ROWS), F32)
    held = lambda *dims: pltpu.VMEM(dims, F32)
    pinned = lambda value: pltpu.with_memory_space_constraint(value, pltpu.HBM)
    parts = pl.pallas_call(
        kernel,
        out_shape=[held(cells, ROWS), held(cells, ROWS), held(8 * PART, ROWS)],
        in_specs=[far, far, far],
        out_specs=[near, near, near],
        scratch_shapes=[
            pltpu.VMEM((cells, ROWS), F32),
            pltpu.VMEM((cells, ROWS), F32),
            pltpu.VMEM((9, CH, CH), F32),
            pltpu.VMEM((COLS + 2, 6 * CH, ROWS), BF16),
            pltpu.VMEM((COLS + 2, 6 * CH, ROWS), BF16),
            pltpu.VMEM((COLS + 2, 3 * CH, ROWS), F32),
            pltpu.VMEM((COLS + 2, 3 * CH, ROWS), F32),
            pltpu.VMEM((CH, ROWS), F32),
            pltpu.VMEM((2, CH, ROWS), F32),
            pltpu.VMEM((2, 2 * CH, ROWS), F32),
            pltpu.VMEM((2, 2 * CH, ROWS), F32),
            pltpu.VMEM((CH, ROWS), F32),
            pltpu.VMEM((2, CH, ROWS), F32),
            pltpu.VMEM((8 * PART, ROWS), F32),
            pltpu.VMEM((8, PART, ROWS), F32),
            pltpu.VMEM((2, 8, THICK, ROWS), F32),
            pltpu.VMEM((2, 8, PART - THICK, ROWS), F32),
            pltpu.SemaphoreType.DMA((3,)),
            pltpu.SemaphoreType.DMA((6,)),
            pltpu.SemaphoreType.DMA((6,)),
            pltpu.SemaphoreType.DMA((6, 8)),
            pltpu.SemaphoreType.DMA((6, 8)),
        ],
        compiler_params=pltpu.CompilerParams(
            collective_id=0, has_side_effects=True, vmem_limit_bytes=40 << 20
        ),
        cost_estimate=pl.CostEstimate(
            flops=3 * 3 * 9 * CH * CH * COLS * ROWS * 2, bytes_accessed=16 * cells * ROWS, transcendentals=0
        ),
    )(pinned(state_field.reshape(cells, ROWS)), pinned(cotangent.reshape(cells, ROWS)), pinned(weight_bank))
    response, grad_field, grad_weight = pl.pallas_call(
        functools.partial(hand_over, 1.0 / math.sqrt(total_cells)),
        out_shape=[field, field, jax.ShapeDtypeStruct((9, CH, CH), F32)],
        in_specs=[near, near, near],
        out_specs=[far, far, far],
        scratch_shapes=[pltpu.VMEM((9, CH, CH), F32), pltpu.SemaphoreType.DMA((3,))],
    )(*[pltpu.with_memory_space_constraint(value, pltpu.VMEM) for value in parts])
    shape = (CH, COLS, ROWS)
    return response.reshape(shape), grad_field.reshape(shape), grad_weight


def solution(mesh):
    in_specs = (P(None, "lon", "lat"), P(), P(None, "lon", "lat"))
    out_specs = (P(None, "lon", "lat"), P(None, "lon", "lat"), P())
    return jax.shard_map(body, mesh=mesh, in_specs=in_specs, out_specs=out_specs, check_vma=False)
```
